32 devices in a mesh: depth: 4 (over y, x), row: 2 (over core), col: 4 (over z).
Axes of the slice: x: 2, y: 2, z: 4, core: 2. Of those that a mesh axis runs over, the one named last changes fastest.
Arguments:
- density: float32 [64, 256, 512], P('depth', 'row', 'col'), may hold values from 0.002 to 0.05
- albedo: bfloat16 [3, 64, 256, 512], P(None, 'depth', 'row', 'col'), may hold values from 0.099609375 to 1
- targets: int32 [2, 4, 2, 4], P(None, None, 'row'), may hold values from -1 to 4, as said below
- offsets: int32 [2, 4, 2, 4], P(None, None, 'row', 'col'), may hold values from 0 to 127
- slab_order: int32 [2, 4], replicated, may hold values from 0 to 3, each once within a row
Outputs:
- frame: float32 [2, 4, 2, 128, 512], P(None, None, 'row', 'depth', 'col')
The draws below stay inside these ranges and needn't reach their ends.
Inputs may be any that keep to these rules, and one draw needn't show every extreme that they name: `targets`: within one view and one row and column c of bricks, the 4 values are c + b, c + b, c + b + 1, c + b + 1, ... assigned to the slabs in some order (two bricks for each value, b is -1 or 0; b is -1 in column 0 and 0 in the last column), so one column of bricks sends at most 4 pieces to one screen tile, a number reached in every view, row and column, and only to tiles c - 1 .. c + 2.
All inputs are finite; a program needn't handle non-finite values.
Results may differ from the reference program's by a relative error of at most 0.0015.
Values may be sent and summed in bfloat16 or wider, within the bound.
No kernel may reach another device: no remote copies, remote signals or barrier semaphores. Data moves between devices by JAX's collectives and lax.ppermute only.
A program may use at most 64 MiB of HBM per device.

```python
import math
import jax
import jax.numpy as jnp
from jax import lax

VIEWS = 2
BD = 16
BR = 128
BC = 128
NZ = 64
NY = 256
NX = 512
N_DEPTH = 4
N_ROW = 2
N_COL = 4


def draw_targets(key, part):
    streams = jax.random.split(jax.random.fold_in(key, 11), 2)
    scores = jax.random.randint(streams[0], (VIEWS, N_ROW, N_COL, N_DEPTH), 0, 1 << 20)
    distinct = scores * N_DEPTH + jnp.arange(N_DEPTH, dtype=jnp.int32)
    ranks = jnp.argsort(jnp.argsort(distinct, axis=-1), axis=-1).astype(jnp.int32)
    relative = ranks // 2
    base_tile = jax.random.randint(streams[1], (VIEWS, N_ROW, N_COL), -1, 1)
    column_ids = jnp.arange(N_COL, dtype=jnp.int32)[None, None, :]
    base_tile = jnp.where(column_ids == 0, -1, base_tile)
    base_tile = jnp.where(column_ids == N_COL - 1, 0, base_tile)
    result = (column_ids + base_tile)[..., None] + relative
    return result.transpose(0, 3, 1, 2).astype(jnp.int32)


def touch_ends(values, stream_key, smallest, largest):
    longest = values.shape.index(max(values.shape))
    spots = []
    for shift in (0, 1):
        where = [jax.random.randint(jax.random.fold_in(stream_key, axis), (), 0, length) for axis, length in enumerate(values.shape)]
        where[longest] = (where[longest] + shift) % values.shape[longest]
        spots.append(tuple(where))
    return values.at[spots[0]].set(smallest).at[spots[1]].set(largest)


def steps_of(key, extent, cuts, smallest, high):
    level, own = 1.0, jax.random.fold_in(key, 6)
    for dim, parts in cuts:
        heights = jnp.exp(jax.random.uniform(jax.random.fold_in(own, dim), (parts,), jnp.float32, smallest / len(cuts), high / len(cuts)))
        level = level * jnp.repeat(heights, extent[dim] // parts).reshape([-1 if axis == dim else 1 for axis in range(len(extent))])
    return level


def setup_inputs(seed: int = 0) -> dict:
    key_of = jax.random.split(jax.random.key(seed), 6)
    density = jnp.clip(jnp.exp(math.log(0.05) - 3.218876 * jax.random.uniform(key_of[0], (NZ, NY, NX), jnp.float32) ** steps_of(key_of[0], (NZ, NY, NX), ((0, 4), (1, 2), (2, 4)), -0.2, 0.2)), 0.002, 0.05)
    albedo = jnp.clip(0.099609375 + 0.9003906 * jax.random.uniform(key_of[1], (3, NZ, NY, NX), jnp.float32) ** steps_of(key_of[1], (3, NZ, NY, NX), ((1, 4), (2, 2), (3, 4)), -0.2, 0.2), 0.099609375, 1.0).astype(jnp.bfloat16)
    targets = draw_targets(jax.random.fold_in(key_of[5], 71), 0)
    offsets = touch_ends(jax.random.randint(key_of[3], (VIEWS, N_DEPTH, N_ROW, N_COL), 0, BC), jax.random.fold_in(key_of[3], 1), 0, BC - 1).astype(jnp.int32)
    slab_order = jax.vmap(lambda own: jax.random.permutation(own, N_DEPTH))(jax.random.split(key_of[4], VIEWS)).reshape((VIEWS, N_DEPTH)).astype(jnp.int32)
    return {"density": density, "albedo": albedo, "targets": targets, "offsets": offsets, "slab_order": slab_order}


SHEARS = (0.3125, -0.4375)
BRIGHTNESS = 4.0


def shear_columns(values, shear, plane_index, margin):
    integer_part = math.floor(shear * plane_index)
    fraction = shear * plane_index - integer_part
    col_count = values.shape[-1]
    padding = [(0, 0)] * (values.ndim - 1) + [(margin, margin)]
    padded = jnp.pad(values, padding)
    nearer = padded[..., margin - integer_part:margin - integer_part + col_count]
    farther = padded[..., margin - integer_part - 1:margin - integer_part - 1 + col_count]
    return (1.0 - fraction) * nearer + fraction * farther


def composite_slabs(premult, shear):
    depth_cells = premult.shape[2]
    colour_sum = jnp.zeros((3,) + premult.shape[1:2] + premult.shape[3:], jnp.float32)
    transmit = jnp.ones(premult.shape[1:2] + premult.shape[3:], jnp.float32)
    for plane_index in range(depth_cells):
        moved = shear_columns(premult[:, :, plane_index], shear, plane_index, depth_cells + 2)
        colour_sum = colour_sum + transmit[None] * moved[:3]
        transmit = transmit * (1.0 - moved[3])
    return jnp.concatenate([colour_sum, (1.0 - transmit)[None]], axis=0).astype(jnp.bfloat16)


def render_row(row_density, row_albedo):
    blocks = row_density.reshape(N_DEPTH, BD, BR, NX)
    slab_plane = jnp.exp(-jnp.sum(blocks, axis=1))
    ahead = jnp.concatenate([jnp.ones((1, BR, NX), jnp.float32), jnp.cumprod(slab_plane, axis=0)[:-1]], axis=0)
    in_front = jnp.cumsum(blocks, axis=1) - blocks
    lighting = ahead[:, None] * jnp.exp(-in_front)
    opacity = 1.0 - jnp.exp(-blocks)
    colour = BRIGHTNESS * row_albedo.reshape(3, N_DEPTH, BD, BR, NX).astype(jnp.float32) * (lighting * opacity)[None]
    premult = jnp.concatenate([colour, opacity[None]], axis=0).reshape(4, N_DEPTH, BD, BR, N_COL, BC)
    return jnp.stack([composite_slabs(premult, shear) for shear in SHEARS])


def place_piece(colour_row, log_row, piece_row, start_col):
    seg_log = lax.dynamic_slice_in_dim(log_row, start_col, BC, 1)
    seg_colour = lax.dynamic_slice_in_dim(colour_row, start_col, BC, 2)
    values = piece_row.astype(jnp.float32)
    seg_colour = seg_colour + jnp.exp(seg_log)[None] * values[:3]
    seg_log = seg_log + jnp.log1p(-values[3])
    return (lax.dynamic_update_slice_in_dim(colour_row, seg_colour, start_col, 2),
            lax.dynamic_update_slice_in_dim(log_row, seg_log, start_col, 1))


def reference(density, albedo, targets, offsets, slab_order):
    row_density = density.reshape(NZ, N_ROW, BR, NX).transpose(1, 0, 2, 3)
    row_albedo = albedo.reshape(3, NZ, N_ROW, BR, NX).transpose(2, 0, 1, 3, 4)
    pictures = lax.map(lambda pair: render_row(pair[0], pair[1]), (row_density, row_albedo))
    pad_width = (N_COL + N_DEPTH + 3) * BC
    frames = []
    for view_index in range(VIEWS):
        view_pictures = pictures[:, view_index]

        def place_step(step_index, state):
            position = step_index // N_COL
            column = step_index % N_COL
            slab = slab_order[view_index, position]
            chosen = lax.dynamic_index_in_dim(view_pictures, slab, axis=2, keepdims=False)
            chosen = lax.dynamic_index_in_dim(chosen, column, axis=3, keepdims=False)
            start_cols = ((targets[view_index, slab, :, column] + 1) * BC + offsets[view_index, slab, :, column]).astype(jnp.int32)
            return jax.vmap(place_piece)(state[0], state[1], chosen, start_cols)

        colour_start = jnp.zeros((N_ROW, 3, BR, pad_width), jnp.float32)
        log_start = jnp.zeros((N_ROW, BR, pad_width), jnp.float32)
        colour_sum, log_sum = lax.fori_loop(0, N_DEPTH * N_COL, place_step, (colour_start, log_start))
        colour_sum = colour_sum[..., BC:BC + NX]
        opacity = 1.0 - jnp.exp(log_sum[..., BC:BC + NX])
        frames.append(jnp.concatenate([colour_sum, opacity[:, None]], axis=1).transpose(1, 0, 2, 3))
    return jnp.stack(frames)
```

```python
import functools
import math

import jax
import jax.numpy as jnp
from jax import lax
from jax.experimental import pallas as pl
from jax.experimental.pallas import tpu as pltpu
from jax.sharding import PartitionSpec as P

SHEARS = (0.3125, -0.4375)
BRIGHTNESS = 4.0
PAIR = 2
VMEM_BYTES = 16 * 1024 * 1024


def plane_steps(shear, depth_cells):
    whole = [math.floor(shear * z) for z in range(depth_cells)]
    return [(k, shear * z - k) for z, k in enumerate(whole)]


def column_shifts(shear, depth_cells):
    found = set()
    for k, f in plane_steps(shear, depth_cells):
        found |= {k, k + 1} if f > 0.0 else {k}
    return sorted(found)


def shift_list(depth_cells):
    return [(v, j) for v, s in enumerate(SHEARS) for j in column_shifts(s, depth_cells)]


def rolled(value, steps):
    size = value.shape[-1]
    steps = steps % size
    return pltpu.roll(value, steps, value.ndim - 1) if steps else value


def plane_kernel(density_ref, plane_ref):
    total = density_ref[0]
    for z in range(1, density_ref.shape[0]):
        total = total + density_ref[z]
    plane_ref[...] = jnp.exp(-total)


def slab_transmittance(density):
    depth_cells, rows, cols = density.shape
    block = min(rows, 32)
    return pl.pallas_call(
        plane_kernel,
        grid=(rows // block,),
        in_specs=[pl.BlockSpec((depth_cells, block, cols), lambda i: (0, i, 0))],
        out_specs=pl.BlockSpec((block, cols), lambda i: (i, 0)),
        out_shape=jax.ShapeDtypeStruct((rows, cols), jnp.float32),
        compiler_params=pltpu.CompilerParams(vmem_limit_bytes=VMEM_BYTES),
        name="slab_plane",
    )(density)


def opacity_weights(k, f, lane, cols):
    if k >= 0:
        inside = lane < cols - k
        return (jnp.where(inside, 1.0 - f, 0.0), jnp.where(inside & (lane >= 1), f, 0.0))
    inside = lane >= -k
    return (jnp.where(inside, 1.0 - f, 0.0), jnp.where(inside | (lane == 0), f, 0.0))


def sums_chunk(density_ref, albedo_ref, sums_ref, opac_ref, rows):
    depth_cells = density_ref.shape[0]
    cols = density_ref.shape[2]
    index = {key: i for i, key in enumerate(shift_list(depth_cells))}
    shape = (rows.size, cols)
    lane = lax.broadcasted_iota(jnp.int32, shape, 1)
    steps = [plane_steps(s, depth_cells) for s in SHEARS]
    transmit = [jnp.ones(shape, jnp.float32) for _ in SHEARS]
    frame = [0 for _ in SHEARS]
    sums = [{} for _ in SHEARS]
    light = jnp.full(shape, BRIGHTNESS, jnp.float32)
    for z in range(depth_cells):
        kept = jnp.exp(-density_ref[z, rows])
        opacity = 1.0 - kept
        lit = light * opacity
        light = light * kept
        farther = rolled(opacity, 1)
        colour = [albedo_ref[c, z, rows].astype(jnp.float32) for c in range(3)]
        for v in range(len(SHEARS)):
            k, f = steps[v][z]
            if frame[v] != k:
                transmit[v] = rolled(transmit[v], frame[v] - k)
                frame[v] = k
            for j, share in ((k, 1.0 - f), (k + 1, f)):
                if share == 0.0:
                    continue
                here = transmit[v] if j == k else rolled(transmit[v], -1)
                weight = here * (lit * share)
                for c in range(3):
                    term = weight * colour[c]
                    sums[v][j, c] = sums[v][j, c] + term if (j, c) in sums[v] else term
            a, b = opacity_weights(k, f, lane, cols)
            moved = a * opacity if f == 0.0 else a * opacity + b * farther
            transmit[v] = transmit[v] * (1.0 - moved)
            following = (steps[v][z + 1][0], steps[v][z + 1][0] + 1) if z + 1 < depth_cells else ()
            for j, c in list(sums[v]):
                if j not in following:
                    sums_ref[index[v, j] * 3 + c, rows] = sums[v].pop((j, c))
    for v in range(len(SHEARS)):
        opac_ref[v, rows] = (1.0 - rolled(transmit[v], frame[v])).astype(opac_ref.dtype)


def sums_kernel(chunk, density_ref, albedo_ref, sums_ref, opac_ref):
    block = density_ref.shape[1]

    def body(i, carry):
        rows = pl.ds(pl.multiple_of(i * chunk, chunk), chunk)
        sums_chunk(density_ref, albedo_ref, sums_ref, opac_ref, rows)
        return carry

    lax.fori_loop(0, block // chunk, body, 0)


def image_sums(density, albedo):
    depth_cells, rows, cols = density.shape
    count = 3 * len(shift_list(depth_cells))
    block = min(rows, 32)
    cells = depth_cells * rows * cols
    return pl.pallas_call(
        functools.partial(sums_kernel, 16),
        grid=(rows // block,),
        in_specs=[
            pl.BlockSpec((depth_cells, block, cols), lambda i: (0, i, 0)),
            pl.BlockSpec((3, depth_cells, block, cols), lambda i: (0, 0, i, 0)),
        ],
        out_specs=[
            pl.BlockSpec((count, block, cols), lambda i: (0, i, 0)),
            pl.BlockSpec((len(SHEARS), block, cols), lambda i: (0, i, 0)),
        ],
        out_shape=[
            jax.ShapeDtypeStruct((count, rows, cols), jnp.float32),
            jax.ShapeDtypeStruct((len(SHEARS), rows, cols), jnp.bfloat16),
        ],
        compiler_params=pltpu.CompilerParams(vmem_limit_bytes=VMEM_BYTES),
        cost_estimate=pl.CostEstimate(
            flops=60 * cells, bytes_accessed=10 * cells + 4 * count * rows * cols, transcendentals=cells
        ),
        name="image_sums",
    )(density, albedo)


def partner(mine, k, count):
    return mine ^ k if count & (count - 1) == 0 else lax.rem(mine + k, count)


def origin(mine, k, count):
    return mine ^ k if count & (count - 1) == 0 else lax.rem(mine - k + count, count)


def swap_depth(value, k, count):
    return lax.ppermute(value, "depth", [(i, int(partner(i, k, count)) if count & (count - 1) == 0 else (i + k) % count) for i in range(count)])


def lit_kernel(slabs, depth_cells, *refs):
    planes, (sums_ref, opac_ref), outs = refs[:slabs], refs[slabs : slabs + 2], refs[slabs + 2 :]
    mine = lax.axis_index("depth")
    strip, cols = outs[0].shape[2:]
    keys = shift_list(depth_cells)
    lane = lax.broadcasted_iota(jnp.int32, (strip, cols), 1)
    for k in range(slabs):
        rows = pl.ds(pl.multiple_of(partner(mine, k, slabs) * strip, strip), strip)
        incoming = jnp.ones((strip, cols), jnp.float32)
        for other in range(1, slabs):
            ahead = origin(mine, other, slabs) < mine
            incoming = incoming * jnp.where(ahead, planes[other][rows], 1.0)
        for v in range(len(SHEARS)):
            for c in range(3):
                total = None
                for i, (view, j) in enumerate(keys):
                    if view != v:
                        continue
                    moved = rolled(incoming * sums_ref[i * 3 + c, rows], j)
                    if j:
                        moved = jnp.where(lane >= j if j > 0 else lane < cols + j, moved, 0.0)
                    total = moved if total is None else total + moved
                outs[k][v, c] = total.astype(jnp.bfloat16)
            outs[k][v, 3] = opac_ref[v, rows]


def lit_strips(planes, sums, opac, depth_cells):
    slabs = len(planes)
    rows, cols = planes[0].shape
    strip = rows // slabs
    vmem = pl.BlockSpec(memory_space=pltpu.VMEM)
    return pl.pallas_call(
        functools.partial(lit_kernel, slabs, depth_cells),
        in_specs=[vmem] * (slabs + 2),
        out_specs=[vmem] * slabs,
        out_shape=[jax.ShapeDtypeStruct((len(SHEARS), 4, strip, cols), jnp.bfloat16)] * slabs,
        compiler_params=pltpu.CompilerParams(vmem_limit_bytes=VMEM_BYTES),
        name="lit_strips",
    )(*planes, sums, opac)


def piece_slots(step, slabs):
    return min(slabs, 2 * PAIR if step < slabs // 2 else PAIR)


def column_swaps(slabs, columns):
    swaps = []
    for step in range(1, slabs // 2 + 1):
        for parity in range(2):
            lefts = [c for c in range(columns - step) if (c // step) % 2 == parity]
            if step > 1 and step == slabs // 2:
                lefts = [c for c in lefts if c > 0]
            if lefts:
                swaps.append((step, parity, lefts))
    return swaps


def swap_columns(value, step, lefts, slabs, columns):
    to = {c: c + step for c in lefts} | {c + step: c for c in lefts}
    pairs = []
    for d in range(slabs):
        for c in range(columns):
            if c in to:
                pairs.append((d * columns + c, d * columns + to[c]))
            elif (d ^ 1) < slabs:
                pairs.append((d * columns + c, (d ^ 1) * columns + c))
    return lax.ppermute(value, ("depth", "col"), pairs)


def covers(targets_ref, view, slab, column, tile):
    first = targets_ref[view, slab, 0, column]
    return (first == tile) | (first + 1 == tile)


def slot_of(targets_ref, view, slab, column, tile, slots, slabs):
    if slots >= slabs:
        return slab
    slot = jnp.int32(0)
    for other in range(slabs):
        ahead = covers(targets_ref, view, other, column, tile) & (other < slab)
        slot = slot + ahead.astype(jnp.int32)
    return jnp.minimum(slot, slots - 1)


def pack_kernel(slabs, columns, swaps, targets_ref, offsets_ref, *refs):
    blocks, outs = refs[:slabs], refs[slabs:]
    mine, column = lax.axis_index("depth"), lax.axis_index("col")
    strip, cols = blocks[0].shape[2:]
    lane = lax.broadcasted_iota(jnp.int32, (4, strip, cols), 2)
    for out in outs:
        out[...] = jnp.zeros_like(out)
    for v in range(len(SHEARS)):
        for k in range(slabs):
            slab = origin(mine, k, slabs)
            first = targets_ref[v, slab, 0, column]
            offset = offsets_ref[v, slab, 0, 0]
            image = blocks[k][v].astype(jnp.float32)
            image = jnp.stack([pltpu.roll(image[c], offset, 1) for c in range(4)])
            left = jnp.where(lane >= offset, image, 0.0).astype(jnp.bfloat16)
            right = jnp.where(lane >= offset, 0.0, image).astype(jnp.bfloat16)
            for out, plan in zip(outs, [None] + swaps, strict=True):
                if plan is None:
                    tile = column
                else:
                    step, parity, _ = plan
                    is_left = lax.rem(lax.div(column, step), 2) == parity
                    tile = column + jnp.where(is_left, step, -step)
                slot = slot_of(targets_ref, v, slab, column, tile, out.shape[1], slabs)

                @pl.when(first == tile)
                def _(out=out, slot=slot, v=v, left=left):
                    out[v, slot] = left

                @pl.when(first + 1 == tile)
                def _(out=out, slot=slot, v=v, right=right):
                    out[v, slot] = right


def packed_pieces(blocks, targets, offsets, columns, swaps):
    slabs = len(blocks)
    views, _, strip, cols = blocks[0].shape
    vmem, smem = pl.BlockSpec(memory_space=pltpu.VMEM), pl.BlockSpec(memory_space=pltpu.SMEM)
    slots = [min(slabs, 2 * PAIR)] + [piece_slots(step, slabs) for step, _, _ in swaps]
    return pl.pallas_call(
        functools.partial(pack_kernel, slabs, columns, swaps),
        in_specs=[smem, smem] + [vmem] * slabs,
        out_specs=[vmem] * len(slots),
        out_shape=[jax.ShapeDtypeStruct((views, n, 4, strip, cols), jnp.bfloat16) for n in slots],
        compiler_params=pltpu.CompilerParams(vmem_limit_bytes=VMEM_BYTES),
        name="pack_pieces",
    )(targets, offsets, *blocks)


def frame_kernel(slabs, columns, swaps, targets_ref, order_ref, own_ref, *refs):
    received, frame_ref = refs[:-1], refs[-1]
    tile = lax.axis_index("col")
    strip, cols = own_ref.shape[3:]
    by_step = {}
    for ref, (step, parity, _) in zip(received, swaps, strict=True):
        by_step.setdefault(step, {})[parity] = ref
    for v in range(len(SHEARS)):
        colour = jnp.zeros((3, strip, cols), jnp.float32)
        weight = jnp.ones((strip, cols), jnp.float32)
        for position in range(slabs):
            slab = order_ref[v, position]
            for step in range(slabs // 2, -2, -1):
                source = tile - step
                present = (source >= 0) & (source < columns)
                column = jnp.clip(source, 0, columns - 1)
                present = present & covers(targets_ref, v, slab, column, tile)
                if step == 0:
                    refs_here = {0: own_ref}
                else:
                    refs_here = by_step.get(abs(step), {})
                if not refs_here:
                    continue
                left = jnp.minimum(source, tile)
                parity = lax.rem(lax.div(jnp.maximum(left, 0), max(abs(step), 1)), 2)
                slots = next(iter(refs_here.values())).shape[1]
                slot = slot_of(targets_ref, v, slab, column, tile, slots, slabs)
                pieces = [refs_here[q][v, slot] for q in sorted(refs_here)]
                piece = pieces[0] if len(pieces) == 1 else jnp.where(parity == 0, pieces[0], pieces[1])
                piece = jnp.where(present, piece.astype(jnp.float32), 0.0)
                colour = colour + weight[None] * piece[:3]
                weight = weight * (1.0 - piece[3])
        frame_ref[v, :3, 0] = colour
        frame_ref[v, 3, 0] = 1.0 - weight


def composed_frame(own, received, targets, slab_order, columns, swaps):
    views, _, _, strip, cols = own.shape
    slabs = slab_order.shape[1]
    vmem, smem = pl.BlockSpec(memory_space=pltpu.VMEM), pl.BlockSpec(memory_space=pltpu.SMEM)
    return pl.pallas_call(
        functools.partial(frame_kernel, slabs, columns, swaps),
        in_specs=[smem, smem] + [vmem] * (1 + len(received)),
        out_specs=vmem,
        out_shape=jax.ShapeDtypeStruct((views, 4, 1, strip, cols), jnp.float32),
        compiler_params=pltpu.CompilerParams(vmem_limit_bytes=VMEM_BYTES),
        name="compose_frame",
    )(targets, slab_order, own, *received)


def on_device(density, albedo, targets, offsets, slab_order):
    depth_cells = density.shape[0]
    slabs, columns = lax.axis_size("depth"), lax.axis_size("col")
    plane = slab_transmittance(density)
    planes = [plane] + [swap_depth(plane, k, slabs) for k in range(1, slabs)]
    sums, opac = image_sums(density, albedo)
    strips = lit_strips(planes, sums, opac, depth_cells)
    blocks = [strips[0]] + [swap_depth(strips[k], k, slabs) for k in range(1, slabs)]
    swaps = column_swaps(slabs, columns)
    own, *outgoing = packed_pieces(blocks, targets, offsets, columns, swaps)
    received = [
        swap_columns(value, step, lefts, slabs, columns)
        for value, (step, _, lefts) in zip(outgoing, swaps, strict=True)
    ]
    return composed_frame(own, received, targets, slab_order, columns, swaps)


def solution(mesh):
    in_specs = (
        P("depth", "row", "col"),
        P(None, "depth", "row", "col"),
        P(None, None, "row", None),
        P(None, None, "row", "col"),
        P(),
    )
    out_specs = P(None, None, "row", "depth", "col")
    return jax.shard_map(
        on_device, mesh=mesh, in_specs=in_specs, out_specs=out_specs, check_vma=False
    )
```

```python
import functools
import math

import jax
import jax.numpy as jnp
from jax import lax
from jax.experimental import pallas as pl
from jax.experimental.pallas import tpu as pltpu
from jax.sharding import PartitionSpec as P

SHEARS = (0.3125, -0.4375)
BRIGHTNESS = 4.0
DENSITY_RANGE = (0.002, 0.05)
CODE_REACH = 76.0
PAIR = 2
VMEM_BYTES = 16 * 1024 * 1024


def plane_steps(shear, depth_cells):
    whole = [math.floor(shear * z) for z in range(depth_cells)]
    return [(k, shear * z - k) for z, k in enumerate(whole)]


def column_shifts(shear, depth_cells):
    found = set()
    for k, f in plane_steps(shear, depth_cells):
        found |= {k, k + 1} if f > 0.0 else {k}
    return sorted(found)


def shift_list(depth_cells):
    return [(v, j) for v, s in enumerate(SHEARS) for j in column_shifts(s, depth_cells)]


def rolled(value, steps):
    size = value.shape[-1]
    steps = steps % size
    return pltpu.roll(value, steps, value.ndim - 1) if steps else value


def depth_code(depth_cells):
    low, high = (depth_cells * d for d in DENSITY_RANGE)
    return 0.5 * (low + high), CODE_REACH / (0.5 * (high - low))


def plane_kernel(parts, density_hbm, code_ref, density_ref, sems):
    depth_cells, rows, _ = density_ref.shape
    block = rows // parts
    middle, spread = depth_code(depth_cells)
    copies = []
    for i in range(parts):
        part = pl.ds(i * block, block)
        copies.append(pltpu.make_async_copy(density_hbm.at[:, part], density_ref.at[:, part], sems.at[i]))
    for copy in copies:
        copy.start()
    for i in range(parts):
        copies[i].wait()
        part = pl.ds(i * block, block)
        total = density_ref[0, part]
        for z in range(1, depth_cells):
            total = total + density_ref[z, part]
        code = jnp.exp(jnp.clip((total - middle) * spread, -CODE_REACH, CODE_REACH))
        code_ref[part] = code.astype(jnp.bfloat16)


def slab_code(density):
    parts = max(1, density.shape[1] // 32)
    return pl.pallas_call(
        functools.partial(plane_kernel, parts),
        in_specs=[pl.BlockSpec(memory_space=pl.ANY)],
        out_specs=[pl.BlockSpec(memory_space=pltpu.VMEM)] * 2,
        out_shape=[
            pltpu.VMEM(density.shape[1:], jnp.bfloat16),
            pltpu.VMEM(density.shape, density.dtype),
        ],
        scratch_shapes=[pltpu.SemaphoreType.DMA((parts,))],
        compiler_params=pltpu.CompilerParams(vmem_limit_bytes=VMEM_BYTES),
        name="slab_code",
    )(pltpu.with_memory_space_constraint(density, pltpu.HBM))


def opacity_weights(k, f, lane, cols):
    if k >= 0:
        inside = lane < cols - k
        return (jnp.where(inside, 1.0 - f, 0.0), jnp.where(inside & (lane >= 1), f, 0.0))
    inside = lane >= -k
    return (jnp.where(inside, 1.0 - f, 0.0), jnp.where(inside | (lane == 0), f, 0.0))


def sums_chunk(density_ref, albedo_ref, sums_ref, opac_ref, rows):
    depth_cells = density_ref.shape[0]
    cols = density_ref.shape[2]
    index = {key: i for i, key in enumerate(shift_list(depth_cells))}
    shape = (rows.size, cols)
    lane = lax.broadcasted_iota(jnp.int32, shape, 1)
    steps = [plane_steps(s, depth_cells) for s in SHEARS]
    transmit = [jnp.ones(shape, jnp.float32) for _ in SHEARS]
    sums = [{} for _ in SHEARS]
    light = jnp.full(shape, BRIGHTNESS, jnp.float32)
    for z in range(depth_cells):
        kept = jnp.exp(-density_ref[z, rows])
        opacity = 1.0 - kept
        lit = light * opacity
        light = light * kept
        farther = rolled(opacity, 1)
        colour = [albedo_ref[c, z, rows].astype(jnp.float32) for c in range(3)]
        for v in range(len(SHEARS)):
            k, f = steps[v][z]
            for j, share in ((k, 1.0 - f), (k + 1, f)):
                if share == 0.0:
                    continue
                weight = rolled(transmit[v], -j) * (lit * share)
                for c in range(3):
                    term = weight * colour[c]
                    sums[v][j, c] = sums[v][j, c] + term if (j, c) in sums[v] else term
            a, b = opacity_weights(k, f, lane, cols)
            moved = a * opacity if f == 0.0 else a * opacity + b * farther
            transmit[v] = transmit[v] * (1.0 - rolled(moved, k))
            following = (steps[v][z + 1][0], steps[v][z + 1][0] + 1) if z + 1 < depth_cells else ()
            for j, c in list(sums[v]):
                if j not in following:
                    total = sums[v].pop((j, c))
                    if j:
                        total = jnp.where(lane < cols - j if j > 0 else lane >= -j, total, 0.0)
                    sums_ref[index[v, j] * 3 + c, rows] = total
    for v in range(len(SHEARS)):
        opac_ref[v, rows] = 1.0 - transmit[v]


def sums_kernel(chunk, parts, density_ref, albedo_hbm, sums_ref, opac_ref, albedo_ref, sems):
    rows = density_ref.shape[1]
    block = rows // parts

    def copy(i):
        part = pl.ds(pl.multiple_of(i * block, block), block)
        return pltpu.make_async_copy(albedo_hbm.at[:, :, part], albedo_ref.at[:, :, part], sems.at[i])

    for i in range(parts):
        copy(i).start()

    def body(i, carry):
        copy(i).wait()
        for part in range(block // chunk):
            at = pl.ds(pl.multiple_of(i * block + part * chunk, chunk), chunk)
            sums_chunk(density_ref, albedo_ref, sums_ref, opac_ref, at)
        return carry

    lax.fori_loop(0, parts, body, 0)


def image_sums(density, albedo):
    depth_cells, rows, cols = density.shape
    count = 3 * len(shift_list(depth_cells))
    chunk = 16
    parts = rows // chunk
    cells = depth_cells * rows * cols
    vmem = pl.BlockSpec(memory_space=pltpu.VMEM)
    return pl.pallas_call(
        functools.partial(sums_kernel, chunk, parts),
        in_specs=[vmem, pl.BlockSpec(memory_space=pl.ANY)],
        out_specs=[vmem, vmem],
        out_shape=[
            pltpu.VMEM((count, rows, cols), jnp.float32),
            pltpu.VMEM((len(SHEARS), rows, cols), jnp.float32),
        ],
        scratch_shapes=[pltpu.VMEM(albedo.shape, albedo.dtype), pltpu.SemaphoreType.DMA((parts,))],
        compiler_params=pltpu.CompilerParams(vmem_limit_bytes=VMEM_BYTES),
        cost_estimate=pl.CostEstimate(
            flops=60 * cells, bytes_accessed=10 * cells + 4 * count * rows * cols, transcendentals=cells
        ),
        name="image_sums",
    )(density, pltpu.with_memory_space_constraint(albedo, pltpu.HBM))


def partner(mine, k, count):
    return mine ^ k if count & (count - 1) == 0 else lax.rem(mine + k, count)


def origin(mine, k, count):
    return mine ^ k if count & (count - 1) == 0 else lax.rem(mine - k + count, count)


def swap_depth(value, k, count):
    return lax.ppermute(value, "depth", [(i, int(partner(i, k, count)) if count & (count - 1) == 0 else (i + k) % count) for i in range(count)])


def lit_kernel(slabs, depth_cells, offsets_any, *refs):
    codes, (sums_ref, opac_ref) = refs[:slabs], refs[slabs : slabs + 2]
    outs, (plain_ref, offsets_ref, sem) = refs[slabs + 2 : -3], refs[-3:]
    fetch = pltpu.make_async_copy(offsets_any, offsets_ref, sem)
    fetch.start()
    mine = lax.axis_index("depth")
    strip, cols = outs[0].shape[2:]
    keys = shift_list(depth_cells)
    middle, spread = depth_code(depth_cells)
    for k in range(slabs):
        rows = pl.ds(pl.multiple_of(partner(mine, k, slabs) * strip, strip), strip)
        ahead_depth = jnp.zeros((strip, cols), jnp.float32)
        for other in range(1, slabs):
            ahead = origin(mine, other, slabs) < mine
            depth = jnp.log(codes[other][rows].astype(jnp.float32)) * (1.0 / spread) + middle
            ahead_depth = ahead_depth + jnp.where(ahead, depth, 0.0)
        incoming = jnp.exp(-ahead_depth)
        for v in range(len(SHEARS)):
            for c in range(3):
                total = None
                for i, (view, j) in enumerate(keys):
                    if view != v:
                        continue
                    moved = rolled(incoming * sums_ref[i * 3 + c, rows], j)
                    total = moved if total is None else total + moved
                plain_ref[k, v, c] = total
    fetch.wait()
    for v in range(len(SHEARS)):
        turn = offsets_ref[v, mine]
        for k in range(slabs):
            rows = pl.ds(pl.multiple_of(partner(mine, k, slabs) * strip, strip), strip)
            for c in range(3):
                outs[k][v, c] = pltpu.roll(plain_ref[k, v, c], turn, 1).astype(jnp.bfloat16)
            outs[k][v, 3] = pltpu.roll(opac_ref[v, rows], turn, 1).astype(jnp.bfloat16)


def lit_strips(codes, sums, opac, offsets, depth_cells):
    slabs = len(codes)
    rows, cols = codes[0].shape
    strip = rows // slabs
    vmem = pl.BlockSpec(memory_space=pltpu.VMEM)
    return pl.pallas_call(
        functools.partial(lit_kernel, slabs, depth_cells),
        in_specs=[pl.BlockSpec(memory_space=pl.ANY)] + [vmem] * (slabs + 2),
        out_specs=[vmem] * slabs,
        out_shape=[jax.ShapeDtypeStruct((len(SHEARS), 4, strip, cols), jnp.bfloat16)] * slabs,
        scratch_shapes=[
            pltpu.VMEM((slabs, len(SHEARS), 3, strip, cols), jnp.float32),
            pltpu.SMEM(offsets.shape, jnp.int32),
            pltpu.SemaphoreType.DMA(()),
        ],
        compiler_params=pltpu.CompilerParams(vmem_limit_bytes=VMEM_BYTES),
        name="lit_strips",
    )(offsets, *codes, sums, opac)


def piece_slots(step, slabs):
    return min(slabs, 2 * PAIR if step < slabs // 2 else PAIR)


def column_swaps(slabs, columns):
    swaps = []
    for step in range(1, slabs // 2 + 1):
        for parity in range(2):
            lefts = [c for c in range(columns - step) if (c // step) % 2 == parity]
            if step > 1 and step == slabs // 2:
                lefts = [c for c in lefts if c > 0]
            if lefts:
                swaps.append((step, parity, lefts))
    return swaps


def swap_columns(value, step, lefts, slabs, columns):
    to = {c: c + step for c in lefts} | {c + step: c for c in lefts}
    rows = lax.axis_size("row")
    pairs = []
    for d in range(slabs):
        for r in range(rows):
            for c in range(columns):
                way = 0 if step == 1 else 0
                there = (d, r, to[c]) if c in to else ((d, r ^ 1, c) if way == 0 else (d ^ way, r, c))
                if there[0] < slabs and there[1] < rows:
                    pairs.append(((d * rows + r) * columns + c, (there[0] * rows + there[1]) * columns + there[2]))
    return lax.ppermute(value, ("depth", "row", "col"), pairs)


def covers(targets_ref, view, slab, column, tile):
    first = targets_ref[view, slab, 0, column]
    return (first == tile) | (first + 1 == tile)


def plan_kernel(slabs, columns, plans, targets_ref, offsets_ref, order_ref, *refs):
    outs = refs[1:]
    mine, column = lax.axis_index("depth"), lax.axis_index("col")
    rows, cols = outs[0].shape[3:]
    lane = lax.broadcasted_iota(jnp.int32, (rows, cols), 1)

    def found_before(view, source, tile):
        count, found = jnp.int32(0), []
        for position in range(slabs):
            first = targets_ref[view, order_ref[view, position], 0, source]
            here = (first == tile) | (first + 1 == tile)
            found.append((here, count))
            count = count + here.astype(jnp.int32)
        return found

    for out, (role, step, parity, lefts, slots) in zip(outs, plans, strict=True):
        if role == "take":
            source = column - step
            present = (source >= 0) & (source < columns)
            source = jnp.clip(source, 0, columns - 1)
            for v in range(len(SHEARS)):
                for position, (here, count) in enumerate(found_before(v, source, column)):
                    for slot in range(slots):
                        chosen = (here & present & (count == slot)).astype(jnp.float32)
                        out[v, position, slot] = jnp.full((rows, cols), chosen).astype(out.dtype)
            continue
        tile = column
        if step:
            is_left = lax.rem(lax.div(column, step), 2) == parity
            is_left = is_left & (column >= lefts[0]) & (column + step < columns)
            is_right = (lax.rem(column, 2) != parity) & (column - step >= lefts[0]) & (step == 1)
            tile = jnp.where(is_left, column + step, jnp.where(is_right, column - step, -PAIR))
        for v in range(len(SHEARS)):
            found = found_before(v, column, tile)
            for k in range(slabs):
                slab = origin(mine, k, slabs)
                first, offset = targets_ref[v, slab, 0, column], offsets_ref[v, slab]
                for slot in range(slots):
                    chosen = jnp.int32(0)
                    for position, (here, count) in enumerate(found):
                        fits = (order_ref[v, position] == slab) & (slot == position)
                        if slots < slabs:
                            fits = (order_ref[v, position] == slab) & here & (count == slot)
                        chosen = chosen + fits.astype(jnp.int32)
                    before = (chosen * (first == tile).astype(jnp.int32)).astype(jnp.float32)
                    after = (chosen * (first + 1 == tile).astype(jnp.int32)).astype(jnp.float32)
                    out[v, slot, k] = jnp.where(lane >= offset, before, after).astype(out.dtype)


def piece_plans(targets, offsets, slab_order, after, columns, plans):
    slabs = slab_order.shape[1]
    views, cols = after.shape[0], after.shape[3]
    vmem, smem = pl.BlockSpec(memory_space=pltpu.VMEM), pl.BlockSpec(memory_space=pltpu.SMEM)
    shapes = []
    for role, _, _, _, slots in plans:
        shapes.append((views, slabs, slots) if role == "take" else (views, slots, slabs))
    return pl.pallas_call(
        functools.partial(plan_kernel, slabs, columns, plans),
        in_specs=[smem, smem, smem, vmem],
        out_specs=[vmem] * len(plans),
        out_shape=[pltpu.VMEM(shape + (16, cols), jnp.bfloat16) for shape in shapes],
        compiler_params=pltpu.CompilerParams(vmem_limit_bytes=VMEM_BYTES),
        name="piece_plans",
    )(targets, offsets, slab_order, after)


def pack_kernel(order, outs_count, *refs):
    slabs = len(order)
    blocks = dict(zip(order, refs[:slabs], strict=True))
    masks, outs = refs[slabs : slabs + outs_count], refs[slabs + outs_count :]
    for mask_ref, out in zip(masks, outs, strict=True):
        views, slots, channels, strip, _ = out.shape
        for v in range(views):
            for slot in range(slots):
                for row in range(0, strip, 16):
                    rows = pl.ds(row, 16)
                    parts = [mask_ref[v, slot, k] for k in range(slabs)]
                    for c in range(channels):
                        total = blocks[0][v, c, rows] * parts[0]
                        for k in range(1, slabs):
                            total = total + blocks[k][v, c, rows] * parts[k]
                        out[v, slot, c, rows] = total


def packed_pieces(blocks, masks, order, name):
    slabs = len(blocks)
    views, channels, strip, cols = blocks[0].shape
    vmem = pl.BlockSpec(memory_space=pltpu.VMEM)
    return pl.pallas_call(
        functools.partial(pack_kernel, order, len(masks)),
        in_specs=[vmem] * (slabs + len(masks)),
        out_specs=[vmem] * len(masks),
        out_shape=[
            jax.ShapeDtypeStruct((views, mask.shape[1], channels, strip, cols), jnp.bfloat16) for mask in masks
        ],
        compiler_params=pltpu.CompilerParams(vmem_limit_bytes=VMEM_BYTES),
        name=name,
    )(*[blocks[k] for k in order], *masks)


def compose_views(slabs, sources, frame_ref):
    strip, cols = frame_ref.shape[3:]
    for v in range(len(SHEARS)):
        colour = [jnp.zeros((strip, cols), jnp.float32) for _ in range(3)]
        weight = jnp.ones((strip, cols), jnp.float32)
        for position in range(slabs):
            for pieces, first, masks in sources:
                slots = pieces[0].shape[1]
                values = []
                for c in range(4):
                    refs = []
                    for ref in pieces:
                        if masks is None:
                            refs.append(ref[v, position, c])
                            continue
                        rows = []
                        for row in range(0, strip, 16):
                            total = ref[v, 0, c, pl.ds(row, 16)] * masks[v, position, 0]
                            for slot in range(1, slots):
                                total = total + ref[v, slot, c, pl.ds(row, 16)] * masks[v, position, slot]
                            rows.append(total)
                        refs.append(jnp.concatenate(rows, axis=0))
                    value = refs[0] if len(refs) == 1 else jnp.where(first, refs[0], refs[1])
                    values.append(value.astype(jnp.float32))
                for c in range(3):
                    colour[c] = colour[c] + weight * values[c]
                weight = weight * (1.0 - values[3])
        for c in range(3):
            frame_ref[v, c, 0] = colour[c]
        frame_ref[v, 3, 0] = 1.0 - weight


def frame_kernel(slabs, swaps, takes, *refs):
    taken, own_ref = dict(zip(takes, refs[: len(takes)], strict=True)), refs[len(takes)]
    received, frame_ref = refs[len(takes) + 1 : -1], refs[-1]
    tile = lax.axis_index("col")
    by_step = {}
    for ref, (step, parity, _) in zip(received, swaps, strict=True):
        by_step.setdefault(step, {})[parity] = ref
    for phase in range(2):
        sources = []
        for step in range(slabs // 2, -2, -1):
            if step == 0:
                sources.append(([own_ref], None, taken.get(step)))
                continue
            refs_here = by_step.get(abs(step), {})
            if abs(step) == 1:
                parity = (phase - step) % 2 if step > 0 else phase
                refs_here = {q: ref for q, ref in refs_here.items() if q == parity}
            if refs_here:
                first = lax.rem(lax.div(tile + step, abs(step)), 2) == 0
                sources.append(([refs_here[q] for q in sorted(refs_here)], first, taken.get(step)))
        pl.when(lax.rem(tile, 2) == phase)(functools.partial(compose_views, slabs, sources, frame_ref))


def composed_frame(own, received, masks, slabs, swaps):
    views, _, channels, strip, cols = own.shape
    vmem = pl.BlockSpec(memory_space=pltpu.VMEM)
    return pl.pallas_call(
        functools.partial(frame_kernel, slabs, swaps, list(masks)),
        in_specs=[vmem] * (len(masks) + 1 + len(received)),
        out_specs=vmem,
        out_shape=jax.ShapeDtypeStruct((views, channels, 1, strip, cols), jnp.float32),
        compiler_params=pltpu.CompilerParams(vmem_limit_bytes=VMEM_BYTES),
        name="compose_frame",
    )(*masks.values(), own, *received)


def on_device(density, albedo, targets, offsets, slab_order):
    depth_cells = density.shape[0]
    slabs, columns = lax.axis_size("depth"), lax.axis_size("col")
    offsets = offsets[:, :, 0, 0]
    code, density = slab_code(density)
    codes = [code] + [swap_depth(code, k, slabs) for k in range(1, slabs)]
    sums, opac = image_sums(density, albedo)
    strips = lit_strips(codes, sums, opac, offsets, depth_cells)
    blocks = [strips[0]] + [swap_depth(strips[k], k, slabs) for k in range(1, slabs)]
    swaps = column_swaps(slabs, columns)
    kept_slots = min(slabs, 2 * PAIR)
    plans = [("send", *swap, piece_slots(swap[0], slabs)) for swap in swaps]
    plans.append(("keep", 0, 0, [], kept_slots))
    takes = []
    for step in [*sorted({step for step, _, _ in swaps}), 0, -1]:
        slots = kept_slots if step == 0 else piece_slots(abs(step), slabs)
        if slots < slabs:
            takes.append(step)
            plans.append(("take", step, 0, [], slots))
    masks = piece_plans(targets, offsets, slab_order, strips[0], columns, plans)
    order = [0, *range(slabs - 1, 0, -1)]
    outgoing = packed_pieces(blocks, masks[: len(swaps)], order, "pack_sent")
    (own,) = packed_pieces(blocks, masks[len(swaps) : len(swaps) + 1], order, "pack_kept")
    received = [
        swap_columns(value, step, lefts, slabs, columns)
        for value, (step, _, lefts) in zip(outgoing, swaps, strict=True)
    ]
    return composed_frame(own, received, dict(zip(takes, masks[len(swaps) + 1 :], strict=True)), slabs, swaps)


def solution(mesh):
    in_specs = (
        P("depth", "row", "col"),
        P(None, "depth", "row", "col"),
        P(None, None, "row", None),
        P(None, None, "row", "col"),
        P(),
    )
    out_specs = P(None, None, "row", "depth", "col")
    return jax.shard_map(
        on_device, mesh=mesh, in_specs=in_specs, out_specs=out_specs, check_vma=False
    )
```

```python
import functools
import math

import jax
import jax.numpy as jnp
from jax import lax
from jax.experimental import pallas as pl
from jax.experimental.pallas import tpu as pltpu
from jax.sharding import PartitionSpec as P

SHEARS = (0.3125, -0.4375)
BRIGHTNESS = 4.0
DENSITY_RANGE = (0.002, 0.05)
CODE_REACH = 76.0
PAIR = 2
VMEM_BYTES = 16 * 1024 * 1024


def plane_steps(shear, depth_cells):
    whole = [math.floor(shear * z) for z in range(depth_cells)]
    return [(k, shear * z - k) for z, k in enumerate(whole)]


def column_shifts(shear, depth_cells):
    found = set()
    for k, f in plane_steps(shear, depth_cells):
        found |= {k, k + 1} if f > 0.0 else {k}
    return sorted(found)


def shift_list(depth_cells):
    return [(v, j) for v, s in enumerate(SHEARS) for j in column_shifts(s, depth_cells)]


def rolled(value, steps):
    size = value.shape[-1]
    steps = steps % size
    return pltpu.roll(value, steps, value.ndim - 1) if steps else value


def depth_code(depth_cells):
    low, high = (depth_cells * d for d in DENSITY_RANGE)
    return 0.5 * (low + high), CODE_REACH / (0.5 * (high - low))


def plane_kernel(parts, density_hbm, code_ref, density_ref, sems):
    depth_cells, rows, _ = density_ref.shape
    block = rows // parts
    middle, spread = depth_code(depth_cells)
    copies = []
    for i in range(parts):
        part = pl.ds(i * block, block)
        copies.append(pltpu.make_async_copy(density_hbm.at[:, part], density_ref.at[:, part], sems.at[i]))
    for copy in copies:
        copy.start()
    for i in range(parts):
        copies[i].wait()
        part = pl.ds(i * block, block)
        total = density_ref[0, part]
        for z in range(1, depth_cells):
            total = total + density_ref[z, part]
        code = jnp.exp(jnp.clip((total - middle) * spread, -CODE_REACH, CODE_REACH))
        code_ref[part] = code.astype(jnp.bfloat16)


def slab_code(density):
    parts = max(1, density.shape[1] // 32)
    return pl.pallas_call(
        functools.partial(plane_kernel, parts),
        in_specs=[pl.BlockSpec(memory_space=pl.ANY)],
        out_specs=[pl.BlockSpec(memory_space=pltpu.VMEM)] * 2,
        out_shape=[
            pltpu.VMEM(density.shape[1:], jnp.bfloat16),
            pltpu.VMEM(density.shape, density.dtype),
        ],
        scratch_shapes=[pltpu.SemaphoreType.DMA((parts,))],
        compiler_params=pltpu.CompilerParams(vmem_limit_bytes=VMEM_BYTES),
        name="slab_code",
    )(pltpu.with_memory_space_constraint(density, pltpu.HBM))


def opacity_weights(k, f, lane, cols):
    if k >= 0:
        inside = lane < cols - k
        return (jnp.where(inside, 1.0 - f, 0.0), jnp.where(inside & (lane >= 1), f, 0.0))
    inside = lane >= -k
    return (jnp.where(inside, 1.0 - f, 0.0), jnp.where(inside | (lane == 0), f, 0.0))


def share_list(depth_cells):
    found = []
    for v, shear in enumerate(SHEARS):
        for z, (k, f) in enumerate(plane_steps(shear, depth_cells)):
            found += [(v, z, j, share) for j, share in ((k, 1.0 - f), (k + 1, f)) if share > 0.0]
    return found


def weigh_rows(density_ref, weights_ref, opac_ref, rows):
    depth_cells, _, cols = density_ref.shape
    tiled = (rows.size // 8, 8, cols)
    lane = lax.broadcasted_iota(jnp.int32, (8, cols), 1)
    shares = share_list(depth_cells)
    steps = [plane_steps(s, depth_cells) for s in SHEARS]
    transmit = [jnp.ones(tiled, jnp.float32) for _ in SHEARS]
    frame = [0 for _ in SHEARS]
    light = jnp.full(tiled, BRIGHTNESS, jnp.float32)
    for z in range(depth_cells):
        kept = jnp.exp(-density_ref[z, rows].reshape(tiled))
        opacity = 1.0 - kept
        lit = light * opacity
        light = light * kept
        farther = rolled(opacity, 1)
        for v in range(len(SHEARS)):
            k, f = steps[v][z]
            transmit[v] = rolled(transmit[v], frame[v] - k)
            frame[v] = k
            for i, (view, plane, j, share) in enumerate(shares):
                if (view, plane) == (v, z):
                    here = transmit[v] if j == k else rolled(transmit[v], -1)
                    weights_ref[i, rows] = (here * (lit * share)).reshape(rows.size, cols)
            a, b = opacity_weights(k, f, lane, cols)
            moved = a[None] * opacity if f == 0.0 else a[None] * opacity + b[None] * farther
            transmit[v] = transmit[v] * (1.0 - moved)
    for v in range(len(SHEARS)):
        opac_ref[v, rows] = (1.0 - rolled(transmit[v], frame[v])).reshape(rows.size, cols).astype(opac_ref.dtype)


def sum_rows(albedo_ref, weights_ref, sums_ref, rows):
    _, depth_cells, _, cols = albedo_ref.shape
    lane = lax.broadcasted_iota(jnp.int32, (8, cols), 1)
    shares = share_list(depth_cells)
    index = {key: i for i, key in enumerate(shift_list(depth_cells))}
    last = {(v, j): z for v, z, j, _ in shares}
    sums = {}
    for z in range(depth_cells):
        colour = [albedo_ref[c, z, rows].astype(jnp.float32) for c in range(3)]
        for i, (v, plane, j, _) in enumerate(shares):
            if plane != z:
                continue
            weight = weights_ref[i, rows]
            for c in range(3):
                term = weight * colour[c]
                total = sums.pop((v, j, c)) + term if (v, j, c) in sums else term
                if last[v, j] > z:
                    sums[v, j, c] = total
                    continue
                if j:
                    inside = lane < cols - j if j > 0 else lane >= -j
                    total = jnp.where(inside[None], total.reshape(-1, 8, cols), 0.0).reshape(total.shape)
                sums_ref[index[v, j] * 3 + c, rows] = total


def sums_kernel(
    chunk, block, density_ref, albedo_hbm, sums_ref, opac_ref, weights_ref, albedo_ref, sems
):
    count = density_ref.shape[1]
    parts = sems.shape[0]

    def copy(i):
        part = pl.ds(i * (count // parts), count // parts)
        return pltpu.make_async_copy(albedo_hbm.at[:, :, part], albedo_ref.at[:, :, part], sems.at[i])

    for i in range(parts):
        copy(i).start()

    def weigh(i, carry):
        weigh_rows(density_ref, weights_ref, opac_ref, pl.ds(pl.multiple_of(i * block, block), block))
        return carry

    def add(i, carry):
        sum_rows(albedo_ref, weights_ref, sums_ref, pl.ds(pl.multiple_of(i * chunk, chunk), chunk))
        return carry

    lax.fori_loop(0, count // block, weigh, 0)
    for i in range(parts):
        copy(i).wait()
    lax.fori_loop(0, count // chunk, add, 0)


def image_sums(density, albedo):
    depth_cells, rows, cols = density.shape
    count = 3 * len(shift_list(depth_cells))
    cells = depth_cells * rows * cols
    vmem = pl.BlockSpec(memory_space=pltpu.VMEM)
    return pl.pallas_call(
        functools.partial(sums_kernel, 16, min(rows, 128)),
        in_specs=[vmem, pl.BlockSpec(memory_space=pl.ANY)],
        out_specs=[vmem, vmem],
        out_shape=[
            pltpu.VMEM((count, rows, cols), jnp.float32),
            pltpu.VMEM((len(SHEARS), rows, cols), jnp.bfloat16),
        ],
        scratch_shapes=[
            pltpu.VMEM((len(share_list(depth_cells)), rows, cols), jnp.float32),
            pltpu.VMEM(albedo.shape, albedo.dtype),
            pltpu.SemaphoreType.DMA((max(1, rows // 32),)),
        ],
        compiler_params=pltpu.CompilerParams(vmem_limit_bytes=VMEM_BYTES),
        cost_estimate=pl.CostEstimate(
            flops=60 * cells, bytes_accessed=10 * cells + 4 * count * rows * cols, transcendentals=cells
        ),
        name="image_sums",
    )(density, pltpu.with_memory_space_constraint(albedo, pltpu.HBM))


def partner(mine, k, count):
    return mine ^ k if count & (count - 1) == 0 else lax.rem(mine + k, count)


def origin(mine, k, count):
    return mine ^ k if count & (count - 1) == 0 else lax.rem(mine - k + count, count)


def swap_depth(value, k, count):
    return lax.ppermute(value, "depth", [(i, int(partner(i, k, count)) if count & (count - 1) == 0 else (i + k) % count) for i in range(count)])


def turn_matrix(offsets, view, slab, cols):
    lane = lax.broadcasted_iota(jnp.int32, offsets.shape, 1)
    row = lax.broadcasted_iota(jnp.int32, offsets.shape, 0)
    own = jnp.where((lane == slab) & (row == view), offsets, 0).astype(jnp.float32)
    offset = jnp.sum(jnp.sum(own, axis=1, keepdims=True), axis=0, keepdims=True).astype(jnp.int32)
    moved = lax.broadcasted_iota(jnp.int32, (cols, cols), 0) + offset
    moved = jnp.where(moved >= cols, moved - cols, moved)
    landing = lax.broadcasted_iota(jnp.int32, (cols, cols), 1)
    return (moved == landing).astype(jnp.float32).astype(jnp.bfloat16)


def lit_kernel(slabs, depth_cells, offsets_ref, *refs):
    codes, (sums_ref, opac_ref), outs = refs[:slabs], refs[slabs : slabs + 2], refs[slabs + 2 :]
    mine = lax.axis_index("depth")
    strip, cols = outs[0].shape[2:]
    keys = shift_list(depth_cells)
    middle, spread = depth_code(depth_cells)
    turns = [turn_matrix(offsets_ref[...], v, mine, cols) for v in range(len(SHEARS))]
    for k in range(slabs):
        rows = pl.ds(pl.multiple_of(partner(mine, k, slabs) * strip, strip), strip)
        ahead_depth = jnp.zeros((strip, cols), jnp.float32)
        for other in range(1, slabs):
            ahead = origin(mine, other, slabs) < mine
            depth = jnp.log(codes[other][rows].astype(jnp.float32)) * (1.0 / spread) + middle
            ahead_depth = ahead_depth + jnp.where(ahead, depth, 0.0)
        incoming = jnp.exp(-ahead_depth)
        for v in range(len(SHEARS)):
            image = []
            for c in range(3):
                total = None
                for i, (view, j) in enumerate(keys):
                    if view != v:
                        continue
                    moved = rolled(incoming * sums_ref[i * 3 + c, rows], j)
                    total = moved if total is None else total + moved
                image.append(total.astype(jnp.bfloat16))
            image = jnp.concatenate([*image, opac_ref[v, rows]], axis=0)
            turned = jnp.dot(image, turns[v], preferred_element_type=jnp.float32)
            outs[k][v] = turned.astype(jnp.bfloat16).reshape(4, strip, cols)


def lit_strips(codes, sums, opac, offsets, depth_cells):
    slabs = len(codes)
    rows, cols = codes[0].shape
    strip = rows // slabs
    vmem = pl.BlockSpec(memory_space=pltpu.VMEM)
    return pl.pallas_call(
        functools.partial(lit_kernel, slabs, depth_cells),
        in_specs=[vmem] * (slabs + 3),
        out_specs=[vmem] * slabs,
        out_shape=[jax.ShapeDtypeStruct((len(SHEARS), 4, strip, cols), jnp.bfloat16)] * slabs,
        compiler_params=pltpu.CompilerParams(vmem_limit_bytes=VMEM_BYTES),
        name="lit_strips",
    )(offsets, *codes, sums, opac)


def piece_slots(step, slabs):
    return min(slabs, 2 * PAIR if step < slabs // 2 else PAIR)


def column_swaps(slabs, columns):
    swaps = []
    for step in range(1, slabs // 2 + 1):
        for parity in range(2):
            lefts = [c for c in range(columns - step) if (c // step) % 2 == parity]
            if step > 1 and step == slabs // 2:
                lefts = [c for c in lefts if c > 0]
            if lefts:
                swaps.append((step, parity, lefts))
    return swaps


def swap_columns(value, step, lefts, slabs, columns):
    to = {c: c + step for c in lefts} | {c + step: c for c in lefts}
    rows = lax.axis_size("row")
    pairs = []
    for d in range(slabs):
        for r in range(rows):
            for c in range(columns):
                way = 0 if step == 1 else 0
                there = (d, r, to[c]) if c in to else ((d, r ^ 1, c) if way == 0 else (d ^ way, r, c))
                if there[0] < slabs and there[1] < rows:
                    pairs.append(((d * rows + r) * columns + c, (there[0] * rows + there[1]) * columns + there[2]))
    return lax.ppermute(value, ("depth", "row", "col"), pairs)


def covers(targets_ref, view, slab, column, tile):
    first = targets_ref[view, slab, 0, column]
    return (first == tile) | (first + 1 == tile)


def plan_kernel(slabs, columns, plans, targets_ref, offsets_ref, order_ref, *refs):
    outs = refs[1:]
    mine, column = lax.axis_index("depth"), lax.axis_index("col")
    rows, cols = outs[0].shape[3:]
    lane = lax.broadcasted_iota(jnp.int32, (rows, cols), 1)

    def found_before(view, source, tile):
        count, found = jnp.int32(0), []
        for position in range(slabs):
            first = targets_ref[view, order_ref[view, position], 0, source]
            here = (first == tile) | (first + 1 == tile)
            found.append((here, count))
            count = count + here.astype(jnp.int32)
        return found

    for out, (role, step, parity, lefts, slots) in zip(outs, plans, strict=True):
        if role == "take":
            source = column - step
            present = (source >= 0) & (source < columns)
            source = jnp.clip(source, 0, columns - 1)
            for v in range(len(SHEARS)):
                for position, (here, count) in enumerate(found_before(v, source, column)):
                    for slot in range(slots):
                        chosen = (here & present & (count == slot)).astype(jnp.float32)
                        out[v, position, slot] = jnp.full((rows, cols), chosen).astype(out.dtype)
            continue
        tile = column
        if step:
            is_left = lax.rem(lax.div(column, step), 2) == parity
            is_left = is_left & (column >= lefts[0]) & (column + step < columns)
            is_right = (lax.rem(column, 2) != parity) & (column - step >= lefts[0]) & (step == 1)
            tile = jnp.where(is_left, column + step, jnp.where(is_right, column - step, -PAIR))
        for v in range(len(SHEARS)):
            found = found_before(v, column, tile)
            for k in range(slabs):
                slab = origin(mine, k, slabs)
                first, offset = targets_ref[v, slab, 0, column], offsets_ref[v, slab]
                for slot in range(slots):
                    chosen = jnp.int32(0)
                    for position, (here, count) in enumerate(found):
                        fits = (order_ref[v, position] == slab) & (slot == position)
                        if slots < slabs:
                            fits = (order_ref[v, position] == slab) & here & (count == slot)
                        chosen = chosen + fits.astype(jnp.int32)
                    before = (chosen * (first == tile).astype(jnp.int32)).astype(jnp.float32)
                    after = (chosen * (first + 1 == tile).astype(jnp.int32)).astype(jnp.float32)
                    out[v, slot, k] = jnp.where(lane >= offset, before, after).astype(out.dtype)


def piece_plans(targets, offsets, slab_order, after, columns, plans):
    slabs = slab_order.shape[1]
    views, cols = after.shape[0], after.shape[3]
    vmem, smem = pl.BlockSpec(memory_space=pltpu.VMEM), pl.BlockSpec(memory_space=pltpu.SMEM)
    shapes = []
    for role, _, _, _, slots in plans:
        shapes.append((views, slabs, slots) if role == "take" else (views, slots, slabs))
    return pl.pallas_call(
        functools.partial(plan_kernel, slabs, columns, plans),
        in_specs=[smem, smem, smem, vmem],
        out_specs=[vmem] * len(plans),
        out_shape=[pltpu.VMEM(shape + (16, cols), jnp.bfloat16) for shape in shapes],
        compiler_params=pltpu.CompilerParams(vmem_limit_bytes=VMEM_BYTES),
        name="piece_plans",
    )(targets, offsets, slab_order, after)


def pack_kernel(order, outs_count, *refs):
    slabs = len(order)
    blocks = dict(zip(order, refs[:slabs], strict=True))
    masks, outs = refs[slabs : slabs + outs_count], refs[slabs + outs_count :]
    for mask_ref, out in zip(masks, outs, strict=True):
        views, slots, channels, strip, _ = out.shape
        for v in range(views):
            for slot in range(slots):
                for row in range(0, strip, 16):
                    rows = pl.ds(row, 16)
                    parts = [mask_ref[v, slot, k] for k in range(slabs)]
                    for c in range(channels):
                        total = blocks[0][v, c, rows] * parts[0]
                        for k in range(1, slabs):
                            total = total + blocks[k][v, c, rows] * parts[k]
                        out[v, slot, c, rows] = total


def packed_pieces(blocks, masks, order, name):
    slabs = len(blocks)
    views, channels, strip, cols = blocks[0].shape
    vmem = pl.BlockSpec(memory_space=pltpu.VMEM)
    return pl.pallas_call(
        functools.partial(pack_kernel, order, len(masks)),
        in_specs=[vmem] * (slabs + len(masks)),
        out_specs=[vmem] * len(masks),
        out_shape=[
            jax.ShapeDtypeStruct((views, mask.shape[1], channels, strip, cols), jnp.bfloat16) for mask in masks
        ],
        compiler_params=pltpu.CompilerParams(vmem_limit_bytes=VMEM_BYTES),
        name=name,
    )(*[blocks[k] for k in order], *masks)


def compose_views(slabs, sources, frame_ref):
    strip, cols = frame_ref.shape[3:]
    for v in range(len(SHEARS)):
        colour = [jnp.zeros((strip, cols), jnp.float32) for _ in range(3)]
        weight = jnp.ones((strip, cols), jnp.float32)
        for position in range(slabs):
            for pieces, first, masks in sources:
                slots = pieces[0].shape[1]
                values = []
                for c in range(4):
                    refs = []
                    for ref in pieces:
                        if masks is None:
                            refs.append(ref[v, position, c])
                            continue
                        rows = []
                        for row in range(0, strip, 16):
                            total = ref[v, 0, c, pl.ds(row, 16)] * masks[v, position, 0]
                            for slot in range(1, slots):
                                total = total + ref[v, slot, c, pl.ds(row, 16)] * masks[v, position, slot]
                            rows.append(total)
                        refs.append(jnp.concatenate(rows, axis=0))
                    value = refs[0] if len(refs) == 1 else jnp.where(first, refs[0], refs[1])
                    values.append(value.astype(jnp.float32))
                for c in range(3):
                    colour[c] = colour[c] + weight * values[c]
                weight = weight * (1.0 - values[3])
        for c in range(3):
            frame_ref[v, c, 0] = colour[c]
        frame_ref[v, 3, 0] = 1.0 - weight


def frame_kernel(slabs, swaps, takes, *refs):
    taken, own_ref = dict(zip(takes, refs[: len(takes)], strict=True)), refs[len(takes)]
    received, frame_ref = refs[len(takes) + 1 : -1], refs[-1]
    tile = lax.axis_index("col")
    by_step = {}
    for ref, (step, parity, _) in zip(received, swaps, strict=True):
        by_step.setdefault(step, {})[parity] = ref
    for phase in range(2):
        sources = []
        for step in range(slabs // 2, -2, -1):
            if step == 0:
                sources.append(([own_ref], None, taken.get(step)))
                continue
            refs_here = by_step.get(abs(step), {})
            if abs(step) == 1:
                parity = (phase - step) % 2 if step > 0 else phase
                refs_here = {q: ref for q, ref in refs_here.items() if q == parity}
            if refs_here:
                first = lax.rem(lax.div(tile + step, abs(step)), 2) == 0
                sources.append(([refs_here[q] for q in sorted(refs_here)], first, taken.get(step)))
        pl.when(lax.rem(tile, 2) == phase)(functools.partial(compose_views, slabs, sources, frame_ref))


def composed_frame(own, received, masks, slabs, swaps):
    views, _, channels, strip, cols = own.shape
    vmem = pl.BlockSpec(memory_space=pltpu.VMEM)
    return pl.pallas_call(
        functools.partial(frame_kernel, slabs, swaps, list(masks)),
        in_specs=[vmem] * (len(masks) + 1 + len(received)),
        out_specs=vmem,
        out_shape=jax.ShapeDtypeStruct((views, channels, 1, strip, cols), jnp.float32),
        compiler_params=pltpu.CompilerParams(vmem_limit_bytes=VMEM_BYTES),
        name="compose_frame",
    )(*masks.values(), own, *received)


def on_device(density, albedo, targets, offsets, slab_order):
    depth_cells = density.shape[0]
    slabs, columns = lax.axis_size("depth"), lax.axis_size("col")
    offsets = offsets[:, :, 0, 0]
    code, density = slab_code(density)
    codes = [code] + [swap_depth(code, k, slabs) for k in range(1, slabs)]
    sums, opac = image_sums(density, albedo)
    strips = lit_strips(codes, sums, opac, offsets, depth_cells)
    blocks = [strips[0]] + [swap_depth(strips[k], k, slabs) for k in range(1, slabs)]
    swaps = column_swaps(slabs, columns)
    kept_slots = min(slabs, 2 * PAIR)
    plans = [("send", *swap, piece_slots(swap[0], slabs)) for swap in swaps]
    plans.append(("keep", 0, 0, [], kept_slots))
    takes = []
    for step in [*sorted({step for step, _, _ in swaps}), 0, -1]:
        slots = kept_slots if step == 0 else piece_slots(abs(step), slabs)
        if slots < slabs:
            takes.append(step)
            plans.append(("take", step, 0, [], slots))
    masks = piece_plans(targets, offsets, slab_order, strips[0], columns, plans)
    order = [0, *range(slabs - 1, 0, -1)]
    outgoing = packed_pieces(blocks, masks[: len(swaps)], order, "pack_sent")
    (own,) = packed_pieces(blocks, masks[len(swaps) : len(swaps) + 1], order, "pack_kept")
    received = [
        swap_columns(value, step, lefts, slabs, columns)
        for value, (step, _, lefts) in zip(outgoing, swaps, strict=True)
    ]
    return composed_frame(own, received, dict(zip(takes, masks[len(swaps) + 1 :], strict=True)), slabs, swaps)


def solution(mesh):
    in_specs = (
        P("depth", "row", "col"),
        P(None, "depth", "row", "col"),
        P(None, None, "row", None),
        P(None, None, "row", "col"),
        P(),
    )
    out_specs = P(None, None, "row", "depth", "col")
    return jax.shard_map(
        on_device, mesh=mesh, in_specs=in_specs, out_specs=out_specs, check_vma=False
    )
```

```python
import functools
import math

import jax
import jax.numpy as jnp
from jax import lax
from jax.experimental import pallas as pl
from jax.experimental.pallas import tpu as pltpu
from jax.sharding import PartitionSpec as P

SHEARS = (0.3125, -0.4375)
BRIGHTNESS = 4.0
DENSITY_RANGE = (0.002, 0.05)
CODE_REACH = 76.0
PAIR = 2
VMEM_BYTES = 16 * 1024 * 1024


def plane_steps(shear, depth_cells):
    whole = [math.floor(shear * z) for z in range(depth_cells)]
    return [(k, shear * z - k) for z, k in enumerate(whole)]


def column_shifts(shear, depth_cells):
    found = set()
    for k, f in plane_steps(shear, depth_cells):
        found |= {k, k + 1} if f > 0.0 else {k}
    return sorted(found)


def shift_list(depth_cells):
    return [(v, j) for v, s in enumerate(SHEARS) for j in column_shifts(s, depth_cells)]


def rolled(value, steps):
    size = value.shape[-1]
    steps = steps % size
    return pltpu.roll(value, steps, value.ndim - 1) if steps else value


def depth_code(depth_cells):
    low, high = (depth_cells * d for d in DENSITY_RANGE)
    return 0.5 * (low + high), CODE_REACH / (0.5 * (high - low))


def plane_kernel(parts, density_hbm, code_ref, density_ref, sems):
    depth_cells, rows, _ = density_ref.shape
    block = rows // parts
    middle, spread = depth_code(depth_cells)
    copies = []
    for i in range(parts):
        part = pl.ds(i * block, block)
        copies.append(pltpu.make_async_copy(density_hbm.at[:, part], density_ref.at[:, part], sems.at[i]))
    for copy in copies:
        copy.start()
    for i in range(parts):
        copies[i].wait()
        part = pl.ds(i * block, block)
        total = density_ref[0, part]
        for z in range(1, depth_cells):
            total = total + density_ref[z, part]
        code = jnp.exp(jnp.clip((total - middle) * spread, -CODE_REACH, CODE_REACH))
        code_ref[part] = code.astype(jnp.bfloat16)


def slab_code(density):
    parts = max(1, density.shape[1] // 32)
    return pl.pallas_call(
        functools.partial(plane_kernel, parts),
        in_specs=[pl.BlockSpec(memory_space=pl.ANY)],
        out_specs=[pl.BlockSpec(memory_space=pltpu.VMEM)] * 2,
        out_shape=[
            pltpu.VMEM(density.shape[1:], jnp.bfloat16),
            pltpu.VMEM(density.shape, density.dtype),
        ],
        scratch_shapes=[pltpu.SemaphoreType.DMA((parts,))],
        compiler_params=pltpu.CompilerParams(vmem_limit_bytes=VMEM_BYTES),
        name="slab_code",
    )(pltpu.with_memory_space_constraint(density, pltpu.HBM))


def opacity_weights(k, f, lane, cols):
    if k >= 0:
        inside = lane < cols - k
        return (jnp.where(inside, 1.0 - f, 0.0), jnp.where(inside & (lane >= 1), f, 0.0))
    inside = lane >= -k
    return (jnp.where(inside, 1.0 - f, 0.0), jnp.where(inside | (lane == 0), f, 0.0))


def share_list(depth_cells):
    found = []
    for v, shear in enumerate(SHEARS):
        for z, (k, f) in enumerate(plane_steps(shear, depth_cells)):
            found += [(v, z, j, share) for j, share in ((k, 1.0 - f), (k + 1, f)) if share > 0.0]
    return found


def weigh_rows(density_ref, weights_ref, opac_ref, rows):
    depth_cells, _, cols = density_ref.shape
    tiled = (rows.size // 8, 8, cols)
    lane = lax.broadcasted_iota(jnp.int32, (8, cols), 1)
    shares = share_list(depth_cells)
    steps = [plane_steps(s, depth_cells) for s in SHEARS]
    transmit = [jnp.ones(tiled, jnp.float32) for _ in SHEARS]
    frame = [0 for _ in SHEARS]
    light = jnp.full(tiled, BRIGHTNESS, jnp.float32)
    for z in range(depth_cells):
        kept = jnp.exp(-density_ref[z, rows].reshape(tiled))
        opacity = 1.0 - kept
        lit = light * opacity
        light = light * kept
        farther = rolled(opacity, 1)
        for v in range(len(SHEARS)):
            k, f = steps[v][z]
            transmit[v] = rolled(transmit[v], frame[v] - k)
            frame[v] = k
            for i, (view, plane, j, share) in enumerate(shares):
                if (view, plane) == (v, z):
                    here = transmit[v] if j == k else rolled(transmit[v], -1)
                    weights_ref[i, rows] = (here * (lit * share)).reshape(rows.size, cols)
            a, b = opacity_weights(k, f, lane, cols)
            moved = a[None] * opacity if f == 0.0 else a[None] * opacity + b[None] * farther
            transmit[v] = transmit[v] * (1.0 - moved)
    for v in range(len(SHEARS)):
        opac_ref[v, rows] = (1.0 - rolled(transmit[v], frame[v])).reshape(rows.size, cols).astype(opac_ref.dtype)


def sum_rows(albedo_ref, weights_ref, sums_ref, rows):
    _, depth_cells, _, cols = albedo_ref.shape
    lane = lax.broadcasted_iota(jnp.int32, (8, cols), 1)
    shares = share_list(depth_cells)
    index = {key: i for i, key in enumerate(shift_list(depth_cells))}
    last = {(v, j): z for v, z, j, _ in shares}
    sums = {}
    for z in range(depth_cells):
        colour = [albedo_ref[c, z, rows].astype(jnp.float32) for c in range(3)]
        for i, (v, plane, j, _) in enumerate(shares):
            if plane != z:
                continue
            weight = weights_ref[i, rows]
            for c in range(3):
                term = weight * colour[c]
                total = sums.pop((v, j, c)) + term if (v, j, c) in sums else term
                if last[v, j] > z:
                    sums[v, j, c] = total
                    continue
                if j:
                    inside = lane < cols - j if j > 0 else lane >= -j
                    total = jnp.where(inside[None], total.reshape(-1, 8, cols), 0.0).reshape(total.shape)
                sums_ref[index[v, j] * 3 + c, rows] = total


def sums_kernel(
    chunk, block, density_ref, albedo_hbm, sums_ref, opac_ref, weights_ref, albedo_ref, sems
):
    count = density_ref.shape[1]
    parts = sems.shape[0]

    def copy(i):
        part = pl.ds(i * (count // parts), count // parts)
        return pltpu.make_async_copy(albedo_hbm.at[:, :, part], albedo_ref.at[:, :, part], sems.at[i])

    for i in range(parts):
        copy(i).start()

    def weigh(i, carry):
        weigh_rows(density_ref, weights_ref, opac_ref, pl.ds(pl.multiple_of(i * block, block), block))
        return carry

    def add(i, carry):
        sum_rows(albedo_ref, weights_ref, sums_ref, pl.ds(pl.multiple_of(i * chunk, chunk), chunk))
        return carry

    lax.fori_loop(0, count // block, weigh, 0)
    for i in range(parts):
        copy(i).wait()
    lax.fori_loop(0, count // chunk, add, 0)


def image_sums(density, albedo):
    depth_cells, rows, cols = density.shape
    count = 3 * len(shift_list(depth_cells))
    cells = depth_cells * rows * cols
    vmem = pl.BlockSpec(memory_space=pltpu.VMEM)
    return pl.pallas_call(
        functools.partial(sums_kernel, 16, min(rows, 128)),
        in_specs=[vmem, pl.BlockSpec(memory_space=pl.ANY)],
        out_specs=[vmem, vmem],
        out_shape=[
            pltpu.VMEM((count, rows, cols), jnp.float32),
            pltpu.VMEM((len(SHEARS), rows, cols), jnp.bfloat16),
        ],
        scratch_shapes=[
            pltpu.VMEM((len(share_list(depth_cells)), rows, cols), jnp.float32),
            pltpu.VMEM(albedo.shape, albedo.dtype),
            pltpu.SemaphoreType.DMA((max(1, rows // 32),)),
        ],
        compiler_params=pltpu.CompilerParams(vmem_limit_bytes=VMEM_BYTES),
        cost_estimate=pl.CostEstimate(
            flops=60 * cells, bytes_accessed=10 * cells + 4 * count * rows * cols, transcendentals=cells
        ),
        name="image_sums",
    )(density, pltpu.with_memory_space_constraint(albedo, pltpu.HBM))


def partner(mine, k, count):
    return mine ^ k if count & (count - 1) == 0 else lax.rem(mine + k, count)


def origin(mine, k, count):
    return mine ^ k if count & (count - 1) == 0 else lax.rem(mine - k + count, count)


def swap_depth(value, k, count):
    return lax.ppermute(value, "depth", [(i, int(partner(i, k, count)) if count & (count - 1) == 0 else (i + k) % count) for i in range(count)])


def turn_matrix(offsets, view, slab, cols):
    lane = lax.broadcasted_iota(jnp.int32, offsets.shape, 1)
    row = lax.broadcasted_iota(jnp.int32, offsets.shape, 0)
    own = jnp.where((lane == slab) & (row == view), offsets, 0).astype(jnp.float32)
    offset = jnp.sum(jnp.sum(own, axis=1, keepdims=True), axis=0, keepdims=True).astype(jnp.int32)
    moved = lax.broadcasted_iota(jnp.int32, (cols, cols), 0) + offset
    moved = jnp.where(moved >= cols, moved - cols, moved)
    landing = lax.broadcasted_iota(jnp.int32, (cols, cols), 1)
    return (moved == landing).astype(jnp.float32).astype(jnp.bfloat16)


def lit_kernel(slabs, depth_cells, chosen, offsets_ref, after_ref, *refs):
    codes, (sums_ref, opac_ref), outs = refs[:slabs], refs[slabs : slabs + 2], refs[slabs + 2 :]
    mine = lax.axis_index("depth")
    strip, cols = outs[0].shape[2:]
    keys = shift_list(depth_cells)
    middle, spread = depth_code(depth_cells)
    turns = [turn_matrix(offsets_ref[...], v, mine, cols) for v in range(len(SHEARS))]
    for k, out in zip(chosen, outs, strict=True):
        rows = pl.ds(pl.multiple_of(partner(mine, k, slabs) * strip, strip), strip)
        ahead_depth = jnp.zeros((strip, cols), jnp.float32)
        for other in range(1, slabs):
            ahead = origin(mine, other, slabs) < mine
            depth = jnp.log(codes[other][rows].astype(jnp.float32)) * (1.0 / spread) + middle
            ahead_depth = ahead_depth + jnp.where(ahead, depth, 0.0)
        incoming = jnp.exp(-ahead_depth)
        for v in range(len(SHEARS)):
            image = []
            for c in range(3):
                total = None
                for i, (view, j) in enumerate(keys):
                    if view != v:
                        continue
                    moved = rolled(incoming * sums_ref[i * 3 + c, rows], j)
                    total = moved if total is None else total + moved
                image.append(total.astype(jnp.bfloat16))
            image = jnp.concatenate([*image, opac_ref[v, rows]], axis=0)
            turned = jnp.dot(image, turns[v], preferred_element_type=jnp.float32)
            out[v] = turned.astype(jnp.bfloat16).reshape(4, strip, cols)


def lit_strips(codes, sums, opac, offsets, after, depth_cells, chosen):
    slabs = len(codes)
    rows, cols = codes[0].shape
    strip = rows // slabs
    vmem = pl.BlockSpec(memory_space=pltpu.VMEM)
    return pl.pallas_call(
        functools.partial(lit_kernel, slabs, depth_cells, chosen),
        in_specs=[vmem, pl.BlockSpec(memory_space=pl.ANY)] + [vmem] * (slabs + 2),
        out_specs=[vmem] * len(chosen),
        out_shape=[jax.ShapeDtypeStruct((len(SHEARS), 4, strip, cols), jnp.bfloat16)] * len(chosen),
        compiler_params=pltpu.CompilerParams(vmem_limit_bytes=VMEM_BYTES),
        name="lit_strips_" + "".join(str(k) for k in chosen),
    )(offsets, after, *codes, sums, opac)


def piece_slots(step, slabs):
    return min(slabs, 2 * PAIR if step < slabs // 2 else PAIR)


def column_swaps(slabs, columns):
    swaps = []
    for step in range(1, slabs // 2 + 1):
        for parity in range(2):
            lefts = [c for c in range(columns - step) if (c // step) % 2 == parity]
            if step > 1 and step == slabs // 2:
                lefts = [c for c in lefts if c > 0]
            if lefts:
                swaps.append((step, parity, lefts))
    return swaps


def swap_columns(value, step, lefts, slabs, columns):
    to = {c: c + step for c in lefts} | {c + step: c for c in lefts}
    rows = lax.axis_size("row")
    pairs = []
    for d in range(slabs):
        for r in range(rows):
            for c in range(columns):
                way = 0 if step == 1 else 0
                there = (d, r, to[c]) if c in to else ((d, r ^ 1, c) if way == 0 else (d ^ way, r, c))
                if there[0] < slabs and there[1] < rows:
                    pairs.append(((d * rows + r) * columns + c, (there[0] * rows + there[1]) * columns + there[2]))
    return lax.ppermute(value, ("depth", "row", "col"), pairs)


def covers(targets_ref, view, slab, column, tile):
    first = targets_ref[view, slab, 0, column]
    return (first == tile) | (first + 1 == tile)


def plan_kernel(slabs, columns, plans, targets_ref, offsets_ref, order_ref, *refs):
    outs = refs[1:]
    mine, column = lax.axis_index("depth"), lax.axis_index("col")
    cols = outs[0].shape[-1]
    shape = (8, cols)
    lane = lax.broadcasted_iota(jnp.int32, shape, 1).astype(jnp.float32)

    def pick(table, row, at):
        rows = lax.broadcasted_iota(jnp.int32, table.shape, 0)
        lanes = lax.broadcasted_iota(jnp.int32, table.shape, 1)
        entry = jnp.where((rows == row) & (lanes == at), table, 0).astype(jnp.float32)
        return jnp.broadcast_to(jnp.sum(jnp.sum(entry, axis=1, keepdims=True), axis=0, keepdims=True), shape)

    def flag(condition):
        return jnp.where(condition, 1.0, 0.0)

    def put(out, at, value):
        out[at] = jnp.concatenate([value, value], axis=0).astype(out.dtype)

    def same(scalar):
        return jnp.full(shape, scalar, jnp.int32).astype(jnp.float32)

    for v in range(len(SHEARS)):
        targets = targets_ref[v, :, 0, :]
        order = [pick(order_ref[...], v, p) for p in range(slabs)]
        slab = [same(origin(mine, k, slabs)) for k in range(slabs)]
        first = [pick(targets, origin(mine, k, slabs), column) for k in range(slabs)]
        offset = [pick(offsets_ref[...], v, origin(mine, k, slabs)) for k in range(slabs)]
        places = [[flag(order[p] == slab[k]) for k in range(slabs)] for p in range(slabs)]

        def columns_of(k, tile):
            return jnp.where(lane >= offset[k], flag(first[k] == tile), flag(first[k] + 1.0 == tile))

        def found_before(firsts, slabs_there, tile):
            count, found = jnp.zeros(shape, jnp.float32), []
            for p in range(slabs):
                here = jnp.zeros(shape, jnp.float32)
                for start, number in zip(firsts, slabs_there, strict=True):
                    covered = flag(start == tile) + flag(start + 1.0 == tile)
                    here = here + flag(order[p] == number) * covered
                found.append((here, count))
                count = count + here
            return found

        for out, (role, step, parity, lefts) in zip(outs, plans, strict=True):
            tile = same(column)
            if role in ("near", "far"):
                is_left = lax.rem(lax.div(column, step), 2) == parity
                is_left = is_left & (column >= lefts[0]) & (column + step < columns)
                is_right = (lax.rem(column, 2) != parity) & (column - step >= lefts[0]) & (step == 1)
                tile = same(jnp.where(is_left, column + step, jnp.where(is_right, column - step, -PAIR)))
            if role == "near":
                for k in range(slabs):
                    put(out, (v, k), columns_of(k, tile))
            elif role == "keep":
                own = [columns_of(k, tile) for k in range(slabs)]
                for p in range(slabs):
                    for k in range(slabs):
                        put(out, (v, p, k), places[p][k] * own[k])
            elif role == "order":
                for p in range(slabs):
                    for k in range(slabs):
                        put(out, (v, p, k), places[p][k])
            elif role == "far":
                found = found_before(first, slab, tile)
                there = [columns_of(k, tile) for k in range(slabs)]
                for slot in range(out.shape[1]):
                    chosen = [here * flag(count == slot) for here, count in found]
                    for k in range(slabs):
                        fits = chosen[0] * places[0][k]
                        for p in range(1, slabs):
                            fits = fits + chosen[p] * places[p][k]
                        put(out, (v, slot, k), fits * there[k])
            elif role == "take":
                source = column - step
                present = same(((source >= 0) & (source < columns)).astype(jnp.int32))
                firsts = [pick(targets, d, source) for d in range(slabs)]
                numbers = [same(d) for d in range(slabs)]
                for p, (here, count) in enumerate(found_before(firsts, numbers, tile)):
                    for slot in range(out.shape[2]):
                        put(out, (v, p, slot), here * present * flag(count == slot))


def piece_plans(targets, offsets, slab_order, columns, after, plans, name):
    slabs = slab_order.shape[1]
    views, cols = len(SHEARS), after.shape[-1]
    vmem = pl.BlockSpec(memory_space=pltpu.VMEM)
    shapes = {"near": lambda n: (slabs,), "far": lambda n: (n, slabs), "take": lambda n: (slabs, n)}
    shapes = [shapes.get(role, lambda n: (slabs, slabs))(piece_slots(step, slabs)) for role, step, _, _ in plans]
    return pl.pallas_call(
        functools.partial(plan_kernel, slabs, columns, plans),
        in_specs=[vmem] * 4,
        out_specs=[vmem] * len(plans),
        out_shape=[pltpu.VMEM((views, *shape, 16, cols), jnp.bfloat16) for shape in shapes],
        compiler_params=pltpu.CompilerParams(vmem_limit_bytes=VMEM_BYTES),
        name=name,
    )(targets, offsets, slab_order, after)


def near_kernel(chosen, outs_count, *refs):
    blocks, masks, outs = refs[: len(chosen)], refs[len(chosen) : -outs_count], refs[-outs_count:]
    for mask_ref, out in zip(masks, outs, strict=True):
        views, _, channels, strip, _ = out.shape
        for v in range(views):
            for i, k in enumerate(chosen):
                mask = mask_ref[v, k]
                for c in range(channels):
                    for row in range(0, strip, 16):
                        rows = pl.ds(row, 16)
                        out[v, i, c, rows] = blocks[i][v, c, rows] * mask


def near_pieces(blocks, masks, chosen, name):
    views, channels, strip, cols = blocks[0].shape
    vmem = pl.BlockSpec(memory_space=pltpu.VMEM)
    return pl.pallas_call(
        functools.partial(near_kernel, chosen, len(masks)),
        in_specs=[vmem] * (len(blocks) + len(masks)),
        out_specs=[vmem] * len(masks),
        out_shape=[jax.ShapeDtypeStruct((views, len(chosen), channels, strip, cols), jnp.bfloat16) for _ in masks],
        compiler_params=pltpu.CompilerParams(vmem_limit_bytes=VMEM_BYTES),
        name=name,
    )(*blocks, *masks)


def pack_kernel(slabs, outs_count, *refs):
    blocks, masks, outs = refs[:slabs], refs[slabs : slabs + outs_count], refs[slabs + outs_count :]
    for mask_ref, out in zip(masks, outs, strict=True):
        views, slots, channels, strip, _ = out.shape
        for v in range(views):
            for slot in range(slots):
                parts = [mask_ref[v, slot, k] for k in range(slabs)]
                for row in range(0, strip, 16):
                    rows = pl.ds(row, 16)
                    for c in range(channels):
                        total = blocks[0][v, c, rows] * parts[0]
                        for k in range(1, slabs):
                            total = total + blocks[k][v, c, rows] * parts[k]
                        out[v, slot, c, rows] = total


def packed_pieces(blocks, masks, name):
    slabs = len(blocks)
    views, channels, strip, cols = blocks[0].shape
    vmem = pl.BlockSpec(memory_space=pltpu.VMEM)
    return pl.pallas_call(
        functools.partial(pack_kernel, slabs, len(masks)),
        in_specs=[vmem] * (slabs + len(masks)),
        out_specs=[vmem] * len(masks),
        out_shape=[
            jax.ShapeDtypeStruct((views, mask.shape[1], channels, strip, cols), jnp.bfloat16) for mask in masks
        ],
        compiler_params=pltpu.CompilerParams(vmem_limit_bytes=VMEM_BYTES),
        name=name,
    )(*blocks, *masks)


def compose_views(sources, order_ref, masks, frame_ref):
    strip, cols = frame_ref.shape[3:]
    slabs = order_ref.shape[1]

    def placed(refs, first, mask_ref, v, p, c):
        pieces = []
        for ref in refs:
            if mask_ref is None:
                pieces.append(ref[v, p, c])
                continue
            parts = []
            for row in range(0, strip, 16):
                rows = pl.ds(row, 16)
                total = ref[v, 0, c, rows] * mask_ref[v, p, 0]
                for slot in range(1, ref.shape[1]):
                    total = total + ref[v, slot, c, rows] * mask_ref[v, p, slot]
                parts.append(total)
            pieces.append(jnp.concatenate(parts, axis=0))
        return pieces[0] if len(pieces) == 1 else jnp.where(first, pieces[0], pieces[1])

    def by_strip(groups, v, p, c):
        parts = []
        for row in range(0, strip, 16):
            rows = pl.ds(row, 16)
            total = None
            for chosen, ref in groups:
                for i, k in enumerate(chosen):
                    term = ref[v, i, c, rows] * order_ref[v, p, k]
                    total = term if total is None else total + term
            parts.append(total)
        return jnp.concatenate(parts, axis=0)

    for v in range(len(SHEARS)):
        colour = [jnp.zeros((strip, cols), jnp.float32) for _ in range(3)]
        weight = jnp.ones((strip, cols), jnp.float32)
        for p in range(slabs):
            for kind, *source in sources:
                take = by_strip if kind == "near" else placed
                values = [take(*source, v, p, c).astype(jnp.float32) for c in range(4)]
                for c in range(3):
                    colour[c] = colour[c] + weight * values[c]
                weight = weight * (1.0 - values[3])
        for c in range(3):
            frame_ref[v, c, 0] = colour[c]
        frame_ref[v, 3, 0] = 1.0 - weight


def frame_kernel(names, slabs, *refs):
    frame_ref = refs[-1]
    given = dict(zip(names, refs[:-1], strict=True))
    tile = lax.axis_index("col")
    near = {parity: [] for parity in range(2)}
    for (kind, *key), ref in given.items():
        if kind == "near":
            near[key[0]].append((key[1], ref))
    for phase in range(2):
        sources = []
        for step in range(slabs // 2, -2, -1):
            if step == 0:
                sources.append(("own", [given["own",]], None, None))
            elif abs(step) == 1:
                groups = near[(phase - step) % 2 if step > 0 else phase]
                if groups:
                    sources.append(("near", groups))
            else:
                arrived = [given["far", step, q] for q in range(2) if ("far", step, q) in given]
                if arrived:
                    first = lax.rem(lax.div(tile + step, step), 2) == 0
                    sources.append(("far", arrived, first, given["take", step]))
        compose = functools.partial(compose_views, sources, given["order",], None, frame_ref)
        pl.when(lax.rem(tile, 2) == phase)(compose)


def composed_frame(given, slabs):
    views, _, channels, strip, cols = given["own",].shape
    vmem = pl.BlockSpec(memory_space=pltpu.VMEM)
    return pl.pallas_call(
        functools.partial(frame_kernel, list(given), slabs),
        in_specs=[vmem] * len(given),
        out_specs=vmem,
        out_shape=jax.ShapeDtypeStruct((views, channels, 1, strip, cols), jnp.float32),
        compiler_params=pltpu.CompilerParams(vmem_limit_bytes=VMEM_BYTES),
        name="compose_frame",
    )(*given.values())


def on_device(density, albedo, targets, offsets, slab_order):
    depth_cells = density.shape[0]
    slabs, columns = lax.axis_size("depth"), lax.axis_size("col")
    offsets = offsets[:, :, 0, 0]
    code, density = slab_code(density)
    codes = [code] + [swap_depth(code, k, slabs) for k in range(1, slabs)]
    sums, opac = image_sums(density, albedo)
    swaps = column_swaps(slabs, columns)
    near = [swap for swap in swaps if swap[0] == 1]
    far = [swap for swap in swaps if swap[0] > 1]
    far_steps = sorted({swap[0] for swap in far})
    roles = [("near", *swap) for swap in near] + [("far", *swap) for swap in far]
    roles += [("take", step, 0, []) for step in far_steps] + [("keep", 0, 0, []), ("order", 0, 0, [])]
    masks = piece_plans(targets, offsets, slab_order, columns, sums, roles, "piece_plans")
    near_masks, masks = masks[: len(near)], masks[len(near) :]
    strips = {}
    for chosen in (list(range(1, slabs)), [0]):
        lit = lit_strips(codes, sums, opac, offsets, offsets, depth_cells, chosen)
        strips |= dict(zip(chosen, lit, strict=True))
    blocks = {0: strips[0]} | {k: swap_depth(strips[k], k, slabs) for k in range(1, slabs)}
    given = {("order",): masks[-1]}
    given |= {("take", step): mask for step, mask in zip(far_steps, masks[len(far) :], strict=False)}
    for name, chosen in (("early", tuple(range(max(1, slabs // 2)))), ("late", tuple(range(max(1, slabs // 2), slabs)))):
        pieces = near_pieces([blocks[k] for k in chosen], near_masks, chosen, "near_pieces_" + name)
        for (step, parity, lefts), piece in zip(near, pieces, strict=True):
            given["near", parity, chosen] = swap_columns(piece, step, lefts, slabs, columns)
    blocks = [blocks[k] for k in range(slabs)]
    if far:
        for (step, parity, lefts), piece in zip(far, packed_pieces(blocks, masks[: len(far)], "far_pieces"), strict=True):
            given["far", step, parity] = swap_columns(piece, step, lefts, slabs, columns)
    (given["own",],) = packed_pieces(blocks, masks[-2:-1], "kept_pieces")
    if slabs == 4:
        names = dict(a=("near", 0, (0, 1)), b=("near", 1, (0, 1)), c=("near", 0, (2, 3)), d=("near", 1, (2, 3)), f=("far", 2, 0))
        first = [names[x] for x in "abfcd"]
        given = {key: given[key] for key in [*first, *(k for k in given if k not in first)]}
    return composed_frame(given, slabs)


def solution(mesh):
    in_specs = (
        P("depth", "row", "col"),
        P(None, "depth", "row", "col"),
        P(None, None, "row", None),
        P(None, None, "row", "col"),
        P(),
    )
    out_specs = P(None, None, "row", "depth", "col")
    return jax.shard_map(
        on_device, mesh=mesh, in_specs=in_specs, out_specs=out_specs, check_vma=False
    )
```

```python
import functools
import math

import jax
import jax.numpy as jnp
from jax import lax
from jax.experimental import pallas as pl
from jax.experimental.pallas import tpu as pltpu
from jax.sharding import PartitionSpec as P

SHEARS = (0.3125, -0.4375)
BRIGHTNESS = 4.0
DENSITY_RANGE = (0.002, 0.05)
CODE_REACH = 76.0
PAIR = 2
VMEM_BYTES = 16 * 1024 * 1024


def plane_steps(shear, depth_cells):
    whole = [math.floor(shear * z) for z in range(depth_cells)]
    return [(k, shear * z - k) for z, k in enumerate(whole)]


def column_shifts(shear, depth_cells):
    found = set()
    for k, f in plane_steps(shear, depth_cells):
        found |= {k, k + 1} if f > 0.0 else {k}
    return sorted(found)


def shift_list(depth_cells):
    return [(v, j) for v, s in enumerate(SHEARS) for j in column_shifts(s, depth_cells)]


def rolled(value, steps):
    size = value.shape[-1]
    steps = steps % size
    return pltpu.roll(value, steps, value.ndim - 1) if steps else value


def depth_code(depth_cells):
    low, high = (depth_cells * d for d in DENSITY_RANGE)
    return 0.5 * (low + high), CODE_REACH / (0.5 * (high - low))


def plane_kernel(parts, density_hbm, code_ref, density_ref, sems):
    depth_cells, rows, _ = density_ref.shape
    block = rows // parts
    middle, spread = depth_code(depth_cells)
    copies = []
    for i in range(parts):
        part = pl.ds(i * block, block)
        copies.append(pltpu.make_async_copy(density_hbm.at[:, part], density_ref.at[:, part], sems.at[i]))
    for copy in copies:
        copy.start()
    for i in range(parts):
        copies[i].wait()
        part = pl.ds(i * block, block)
        total = density_ref[0, part]
        for z in range(1, depth_cells):
            total = total + density_ref[z, part]
        code = jnp.exp(jnp.clip((total - middle) * spread, -CODE_REACH, CODE_REACH))
        code_ref[part] = code.astype(jnp.bfloat16)


def slab_code(density):
    parts = max(1, density.shape[1] // 32)
    return pl.pallas_call(
        functools.partial(plane_kernel, parts),
        in_specs=[pl.BlockSpec(memory_space=pl.ANY)],
        out_specs=[pl.BlockSpec(memory_space=pltpu.VMEM)] * 2,
        out_shape=[
            pltpu.VMEM(density.shape[1:], jnp.bfloat16),
            pltpu.VMEM(density.shape, density.dtype),
        ],
        scratch_shapes=[pltpu.SemaphoreType.DMA((parts,))],
        compiler_params=pltpu.CompilerParams(vmem_limit_bytes=VMEM_BYTES),
        name="slab_code",
    )(pltpu.with_memory_space_constraint(density, pltpu.HBM))


def opacity_weights(k, f, lane, cols):
    if k >= 0:
        inside = lane < cols - k
        return (jnp.where(inside, 1.0 - f, 0.0), jnp.where(inside & (lane >= 1), f, 0.0))
    inside = lane >= -k
    return (jnp.where(inside, 1.0 - f, 0.0), jnp.where(inside | (lane == 0), f, 0.0))


def share_list(depth_cells):
    found = []
    for v, shear in enumerate(SHEARS):
        for z, (k, f) in enumerate(plane_steps(shear, depth_cells)):
            found += [(v, z, j, share) for j, share in ((k, 1.0 - f), (k + 1, f)) if share > 0.0]
    return found


def weigh_rows(density_ref, weights_ref, opac_ref, rows):
    depth_cells, _, cols = density_ref.shape
    tiled = (rows.size // 8, 8, cols)
    lane = lax.broadcasted_iota(jnp.int32, (8, cols), 1)
    shares = share_list(depth_cells)
    steps = [plane_steps(s, depth_cells) for s in SHEARS]
    transmit = [jnp.ones(tiled, jnp.float32) for _ in SHEARS]
    frame = [0 for _ in SHEARS]
    light = jnp.full(tiled, BRIGHTNESS, jnp.float32)
    for z in range(depth_cells):
        kept = jnp.exp(-density_ref[z, rows].reshape(tiled))
        opacity = 1.0 - kept
        lit = light * opacity
        light = light * kept
        farther = rolled(opacity, 1)
        for v in range(len(SHEARS)):
            k, f = steps[v][z]
            transmit[v] = rolled(transmit[v], frame[v] - k)
            frame[v] = k
            for i, (view, plane, j, share) in enumerate(shares):
                if (view, plane) == (v, z):
                    here = transmit[v] if j == k else rolled(transmit[v], -1)
                    weights_ref[i, rows] = (here * (lit * share)).reshape(rows.size, cols)
            a, b = opacity_weights(k, f, lane, cols)
            moved = a[None] * opacity if f == 0.0 else a[None] * opacity + b[None] * farther
            transmit[v] = transmit[v] * (1.0 - moved)
    for v in range(len(SHEARS)):
        opac_ref[v, rows] = (1.0 - rolled(transmit[v], frame[v])).reshape(rows.size, cols).astype(opac_ref.dtype)


def sum_rows(albedo_ref, weights_ref, sums_ref, rows):
    _, depth_cells, _, cols = albedo_ref.shape
    lane = lax.broadcasted_iota(jnp.int32, (8, cols), 1)
    shares = share_list(depth_cells)
    index = {key: i for i, key in enumerate(shift_list(depth_cells))}
    last = {(v, j): z for v, z, j, _ in shares}
    sums = {}
    for z in range(depth_cells):
        colour = [albedo_ref[c, z, rows].astype(jnp.float32) for c in range(3)]
        for i, (v, plane, j, _) in enumerate(shares):
            if plane != z:
                continue
            weight = weights_ref[i, rows]
            for c in range(3):
                term = weight * colour[c]
                total = sums.pop((v, j, c)) + term if (v, j, c) in sums else term
                if last[v, j] > z:
                    sums[v, j, c] = total
                    continue
                if j:
                    inside = lane < cols - j if j > 0 else lane >= -j
                    total = jnp.where(inside[None], total.reshape(-1, 8, cols), 0.0).reshape(total.shape)
                sums_ref[index[v, j] * 3 + c, rows] = total


def sums_kernel(
    chunk, block, density_ref, albedo_hbm, sums_ref, opac_ref, weights_ref, albedo_ref, sems
):
    count = density_ref.shape[1]
    parts = sems.shape[0]

    def copy(i):
        part = pl.ds(i * (count // parts), count // parts)
        return pltpu.make_async_copy(albedo_hbm.at[:, :, part], albedo_ref.at[:, :, part], sems.at[i])

    for i in range(parts):
        copy(i).start()

    def weigh(i, carry):
        weigh_rows(density_ref, weights_ref, opac_ref, pl.ds(pl.multiple_of(i * block, block), block))
        return carry

    def add(i, carry):
        sum_rows(albedo_ref, weights_ref, sums_ref, pl.ds(pl.multiple_of(i * chunk, chunk), chunk))
        return carry

    lax.fori_loop(0, count // block, weigh, 0)
    for i in range(parts):
        copy(i).wait()
    lax.fori_loop(0, count // chunk, add, 0)


def image_sums(density, albedo):
    depth_cells, rows, cols = density.shape
    count = 3 * len(shift_list(depth_cells))
    cells = depth_cells * rows * cols
    vmem = pl.BlockSpec(memory_space=pltpu.VMEM)
    return pl.pallas_call(
        functools.partial(sums_kernel, 16, min(rows, 128)),
        in_specs=[vmem, pl.BlockSpec(memory_space=pl.ANY)],
        out_specs=[vmem, vmem],
        out_shape=[
            pltpu.VMEM((count, rows, cols), jnp.float32),
            pltpu.VMEM((len(SHEARS), rows, cols), jnp.bfloat16),
        ],
        scratch_shapes=[
            pltpu.VMEM((len(share_list(depth_cells)), rows, cols), jnp.float32),
            pltpu.VMEM(albedo.shape, albedo.dtype),
            pltpu.SemaphoreType.DMA((max(1, rows // 32),)),
        ],
        compiler_params=pltpu.CompilerParams(vmem_limit_bytes=VMEM_BYTES),
        cost_estimate=pl.CostEstimate(
            flops=60 * cells, bytes_accessed=10 * cells + 4 * count * rows * cols, transcendentals=cells
        ),
        name="image_sums",
    )(density, pltpu.with_memory_space_constraint(albedo, pltpu.HBM))


def partner(mine, k, count):
    return mine ^ k if count & (count - 1) == 0 else lax.rem(mine + k, count)


def origin(mine, k, count):
    return mine ^ k if count & (count - 1) == 0 else lax.rem(mine - k + count, count)


def swap_depth(value, k, count):
    return lax.ppermute(value, "depth", [(i, int(partner(i, k, count)) if count & (count - 1) == 0 else (i + k) % count) for i in range(count)])


def turn_matrix(offsets, view, slab, cols):
    lane = lax.broadcasted_iota(jnp.int32, offsets.shape, 1)
    row = lax.broadcasted_iota(jnp.int32, offsets.shape, 0)
    own = jnp.where((lane == slab) & (row == view), offsets, 0).astype(jnp.float32)
    offset = jnp.sum(jnp.sum(own, axis=1, keepdims=True), axis=0, keepdims=True).astype(jnp.int32)
    moved = lax.broadcasted_iota(jnp.int32, (cols, cols), 0) + offset
    moved = jnp.where(moved >= cols, moved - cols, moved)
    landing = lax.broadcasted_iota(jnp.int32, (cols, cols), 1)
    return (moved == landing).astype(jnp.float32).astype(jnp.bfloat16)


def lit_kernel(slabs, depth_cells, chosen, offsets_ref, after_ref, *refs):
    codes, (sums_ref, opac_ref), outs = refs[:slabs], refs[slabs : slabs + 2], refs[slabs + 2 :]
    codes = [codes[-k % slabs] for k in range(slabs)]
    mine = lax.axis_index("depth")
    strip, cols = outs[0].shape[2:]
    keys = shift_list(depth_cells)
    middle, spread = depth_code(depth_cells)
    turns = [turn_matrix(offsets_ref[...], v, mine, cols) for v in range(len(SHEARS))]
    for k, out in zip(chosen, outs, strict=True):
        rows = pl.ds(pl.multiple_of(partner(mine, k, slabs) * strip, strip), strip)
        ahead_depth = jnp.zeros((strip, cols), jnp.float32)
        for other in range(1, slabs):
            ahead = origin(mine, other, slabs) < mine
            depth = jnp.log(codes[other][rows].astype(jnp.float32)) * (1.0 / spread) + middle
            ahead_depth = ahead_depth + jnp.where(ahead, depth, 0.0)
        incoming = jnp.exp(-ahead_depth)
        for v in range(len(SHEARS)):
            image = []
            for c in range(3):
                total = None
                for i, (view, j) in enumerate(keys):
                    if view != v:
                        continue
                    moved = rolled(incoming * sums_ref[i * 3 + c, rows], j)
                    total = moved if total is None else total + moved
                image.append(total.astype(jnp.bfloat16))
            image = jnp.concatenate([*image, opac_ref[v, rows]], axis=0)
            turned = jnp.dot(image, turns[v], preferred_element_type=jnp.float32)
            out[v] = turned.astype(jnp.bfloat16).reshape(4, strip, cols)


def lit_strips(codes, sums, opac, offsets, after, depth_cells, chosen):
    slabs = len(codes)
    rows, cols = codes[0].shape
    strip = rows // slabs
    vmem = pl.BlockSpec(memory_space=pltpu.VMEM)
    return pl.pallas_call(
        functools.partial(lit_kernel, slabs, depth_cells, chosen),
        in_specs=[vmem, pl.BlockSpec(memory_space=pl.ANY)] + [vmem] * (slabs + 2),
        out_specs=[vmem] * len(chosen),
        out_shape=[jax.ShapeDtypeStruct((len(SHEARS), 4, strip, cols), jnp.bfloat16)] * len(chosen),
        compiler_params=pltpu.CompilerParams(vmem_limit_bytes=VMEM_BYTES),
        name="lit_strips_" + "".join(str(k) for k in chosen),
    )(offsets, after, *[codes[-k % slabs] for k in range(slabs)], sums, opac)


def piece_slots(step, slabs):
    return min(slabs, 2 * PAIR if step < slabs // 2 else PAIR)


def column_swaps(slabs, columns):
    swaps = []
    for step in range(1, slabs // 2 + 1):
        for parity in range(2):
            lefts = [c for c in range(columns - step) if (c // step) % 2 == parity]
            if step > 1 and step == slabs // 2:
                lefts = [c for c in lefts if c > 0]
            if lefts:
                swaps.append((step, parity, lefts))
    return swaps


def swap_columns(value, step, lefts, slabs, columns):
    to = {c: c + step for c in lefts} | {c + step: c for c in lefts}
    rows = lax.axis_size("row")
    pairs = []
    for d in range(slabs):
        for r in range(rows):
            for c in range(columns):
                way = 0 if step == 1 else 0
                there = (d, r, to[c]) if c in to else ((d, r ^ 1, c) if way == 0 else (d ^ way, r, c))
                if there[0] < slabs and there[1] < rows:
                    pairs.append(((d * rows + r) * columns + c, (there[0] * rows + there[1]) * columns + there[2]))
    return lax.ppermute(value, ("depth", "row", "col"), pairs)


def covers(targets_ref, view, slab, column, tile):
    first = targets_ref[view, slab, 0, column]
    return (first == tile) | (first + 1 == tile)


def plan_kernel(slabs, columns, plans, targets_ref, offsets_ref, order_ref, *refs):
    outs = refs[1:]
    mine, column = lax.axis_index("depth"), lax.axis_index("col")
    cols = outs[0].shape[-1]
    shape = (8, cols)
    lane = lax.broadcasted_iota(jnp.int32, shape, 1).astype(jnp.float32)

    def pick(table, row, at):
        rows = lax.broadcasted_iota(jnp.int32, table.shape, 0)
        lanes = lax.broadcasted_iota(jnp.int32, table.shape, 1)
        entry = jnp.where((rows == row) & (lanes == at), table, 0).astype(jnp.float32)
        return jnp.broadcast_to(jnp.sum(jnp.sum(entry, axis=1, keepdims=True), axis=0, keepdims=True), shape)

    def flag(condition):
        return jnp.where(condition, 1.0, 0.0)

    def put(out, at, value):
        out[at] = jnp.concatenate([value, value], axis=0).astype(out.dtype)

    def same(scalar):
        return jnp.full(shape, scalar, jnp.int32).astype(jnp.float32)

    for v in range(len(SHEARS)):
        targets = targets_ref[v, :, 0, :]
        order = [pick(order_ref[...], v, p) for p in range(slabs)]
        slab = [same(origin(mine, k, slabs)) for k in range(slabs)]
        first = [pick(targets, origin(mine, k, slabs), column) for k in range(slabs)]
        offset = [pick(offsets_ref[...], v, origin(mine, k, slabs)) for k in range(slabs)]
        places = [[flag(order[p] == slab[k]) for k in range(slabs)] for p in range(slabs)]

        def columns_of(k, tile):
            return jnp.where(lane >= offset[k], flag(first[k] == tile), flag(first[k] + 1.0 == tile))

        def found_before(firsts, slabs_there, tile):
            count, found = jnp.zeros(shape, jnp.float32), []
            for p in range(slabs):
                here = jnp.zeros(shape, jnp.float32)
                for start, number in zip(firsts, slabs_there, strict=True):
                    covered = flag(start == tile) + flag(start + 1.0 == tile)
                    here = here + flag(order[p] == number) * covered
                found.append((here, count))
                count = count + here
            return found

        for out, (role, step, parity, lefts) in zip(outs, plans, strict=True):
            tile = same(column)
            if role in ("near", "far"):
                is_left = lax.rem(lax.div(column, step), 2) == parity
                is_left = is_left & (column >= lefts[0]) & (column + step < columns)
                is_right = (lax.rem(column, 2) != parity) & (column - step >= lefts[0]) & (step == 1)
                tile = same(jnp.where(is_left, column + step, jnp.where(is_right, column - step, -PAIR)))
            if role == "near":
                for k in range(slabs):
                    put(out, (v, k), columns_of(k, tile))
            elif role == "keep":
                own = [columns_of(k, tile) for k in range(slabs)]
                for p in range(slabs):
                    for k in range(slabs):
                        put(out, (v, p, k), places[p][k] * own[k])
            elif role == "order":
                for p in range(slabs):
                    for k in range(slabs):
                        put(out, (v, p, k), places[p][k])
            elif role == "far":
                found = found_before(first, slab, tile)
                there = [columns_of(k, tile) for k in range(slabs)]
                for slot in range(out.shape[1]):
                    chosen = [here * flag(count == slot) for here, count in found]
                    for k in range(slabs):
                        fits = chosen[0] * places[0][k]
                        for p in range(1, slabs):
                            fits = fits + chosen[p] * places[p][k]
                        put(out, (v, slot, k), fits * there[k])
            elif role == "take":
                source = column - step
                present = same(((source >= 0) & (source < columns)).astype(jnp.int32))
                firsts = [pick(targets, d, source) for d in range(slabs)]
                numbers = [same(d) for d in range(slabs)]
                for p, (here, count) in enumerate(found_before(firsts, numbers, tile)):
                    for slot in range(out.shape[2]):
                        put(out, (v, p, slot), here * present * flag(count == slot))


def piece_plans(targets, offsets, slab_order, columns, after, plans, name):
    slabs = slab_order.shape[1]
    views, cols = len(SHEARS), after.shape[-1]
    vmem = pl.BlockSpec(memory_space=pltpu.VMEM)
    shapes = {"near": lambda n: (slabs,), "far": lambda n: (n, slabs), "take": lambda n: (slabs, n)}
    shapes = [shapes.get(role, lambda n: (slabs, slabs))(piece_slots(step, slabs)) for role, step, _, _ in plans]
    return pl.pallas_call(
        functools.partial(plan_kernel, slabs, columns, plans),
        in_specs=[vmem] * 4,
        out_specs=[vmem] * len(plans),
        out_shape=[pltpu.VMEM((views, *shape, 16, cols), jnp.bfloat16) for shape in shapes],
        compiler_params=pltpu.CompilerParams(vmem_limit_bytes=VMEM_BYTES),
        name=name,
    )(targets, offsets, slab_order, after)


def near_kernel(chosen, outs_count, *refs):
    blocks, masks, outs = refs[: len(chosen)], refs[len(chosen) : -outs_count], refs[-outs_count:]
    for mask_ref, out in zip(masks, outs, strict=True):
        views, _, channels, strip, _ = out.shape
        for v in range(views):
            for i, k in enumerate(chosen):
                mask = mask_ref[v, k]
                for c in range(channels):
                    for row in range(0, strip, 16):
                        rows = pl.ds(row, 16)
                        out[v, i, c, rows] = blocks[i][v, c, rows] * mask


def near_pieces(blocks, masks, chosen, name):
    views, channels, strip, cols = blocks[0].shape
    vmem = pl.BlockSpec(memory_space=pltpu.VMEM)
    return pl.pallas_call(
        functools.partial(near_kernel, chosen, len(masks)),
        in_specs=[vmem] * (len(blocks) + len(masks)),
        out_specs=[vmem] * len(masks),
        out_shape=[jax.ShapeDtypeStruct((views, len(chosen), channels, strip, cols), jnp.bfloat16) for _ in masks],
        compiler_params=pltpu.CompilerParams(vmem_limit_bytes=VMEM_BYTES),
        name=name,
    )(*blocks, *masks)


def pack_kernel(slabs, outs_count, *refs):
    blocks, masks, outs = refs[:slabs], refs[slabs : slabs + outs_count], refs[slabs + outs_count :]
    for mask_ref, out in zip(masks, outs, strict=True):
        views, slots, channels, strip, _ = out.shape
        for v in range(views):
            for slot in range(slots):
                parts = [mask_ref[v, slot, k] for k in range(slabs)]
                for row in range(0, strip, 16):
                    rows = pl.ds(row, 16)
                    for c in range(channels):
                        total = blocks[0][v, c, rows] * parts[0]
                        for k in range(1, slabs):
                            total = total + blocks[k][v, c, rows] * parts[k]
                        out[v, slot, c, rows] = total


def packed_pieces(blocks, masks, name):
    slabs = len(blocks)
    views, channels, strip, cols = blocks[0].shape
    vmem = pl.BlockSpec(memory_space=pltpu.VMEM)
    return pl.pallas_call(
        functools.partial(pack_kernel, slabs, len(masks)),
        in_specs=[vmem] * (slabs + len(masks)),
        out_specs=[vmem] * len(masks),
        out_shape=[
            jax.ShapeDtypeStruct((views, mask.shape[1], channels, strip, cols), jnp.bfloat16) for mask in masks
        ],
        compiler_params=pltpu.CompilerParams(vmem_limit_bytes=VMEM_BYTES),
        name=name,
    )(*blocks, *masks)


def blend_kernel(names, *refs):
    given, out = dict(zip(names, refs[:-1], strict=True)), refs[-1]
    views, slabs, _, strip, cols = out.shape
    order_ref = given["order",]
    tile = lax.axis_index("col")
    near = {parity: [] for parity in range(2)}
    for (kind, *key), ref in given.items():
        if kind == "near":
            near[key[0]].append((key[1], ref))

    def by_strip(groups, v, p, c, rows):
        total = None
        for chosen, ref in groups:
            for i, k in enumerate(chosen):
                term = ref[v, i, c, rows] * order_ref[v, p, k]
                total = term if total is None else total + term
        return total

    def blend(left, right):
        for v in range(views):
            for p in range(slabs):
                for row in range(0, strip, 16):
                    rows = pl.ds(row, 16)
                    colour = [jnp.zeros((16, cols), jnp.float32) for _ in range(3)]
                    through = jnp.ones((16, cols), jnp.float32)
                    for source in (left, None, right):
                        if source is None:
                            values = [given["own",][v, p, c, rows] for c in range(4)]
                        elif source:
                            values = [by_strip(source, v, p, c, rows) for c in range(4)]
                        else:
                            continue
                        values = [value.astype(jnp.float32) for value in values]
                        for c in range(3):
                            colour[c] = colour[c] + through * values[c]
                        through = through * (1.0 - values[3])
                    for c in range(3):
                        out[v, p, c, rows] = colour[c]
                    out[v, p, 3, rows] = through

    for phase in range(2):
        pl.when(lax.rem(tile, 2) == phase)(functools.partial(blend, near[(phase - 1) % 2], near[phase]))


def blended_pieces(given, slabs):
    views, _, channels, strip, cols = given["own",].shape
    vmem = pl.BlockSpec(memory_space=pltpu.VMEM)
    return pl.pallas_call(
        functools.partial(blend_kernel, list(given)),
        in_specs=[vmem] * len(given),
        out_specs=vmem,
        out_shape=pltpu.VMEM((views, slabs, channels, strip, cols), jnp.float32),
        compiler_params=pltpu.CompilerParams(vmem_limit_bytes=VMEM_BYTES),
        name="blend_pieces",
    )(*given.values())


def frame_kernel(names, *refs):
    blended_ref, given = refs[0], dict(zip(names, refs[1:-3], strict=True))
    frame_hbm, frame_ref, sems = refs[-3:]
    views, slabs, _, strip, cols = blended_ref.shape
    tile = lax.axis_index("col")
    steps = sorted({key[1] for key in given if key[0] == "take"}, reverse=True)

    def placed(step, v, p, c, rows):
        arrived = [given["far", step, q] for q in range(2) if ("far", step, q) in given]
        pieces = []
        for ref in arrived:
            total = ref[v, 0, c, rows] * given["take", step][v, p, 0]
            for slot in range(1, ref.shape[1]):
                total = total + ref[v, slot, c, rows] * given["take", step][v, p, slot]
            pieces.append(total)
        first = lax.rem(lax.div(tile + step, step), 2) == 0
        return pieces[0] if len(pieces) == 1 else jnp.where(first, pieces[0], pieces[1])

    copies = []
    for v in range(views):
        for row in range(0, strip, 16):
            rows = pl.ds(row, 16)
            colour = [jnp.zeros((16, cols), jnp.float32) for _ in range(3)]
            weight = jnp.ones((16, cols), jnp.float32)
            for p in range(slabs):
                for step in steps:
                    values = [placed(step, v, p, c, rows).astype(jnp.float32) for c in range(4)]
                    for c in range(3):
                        colour[c] = colour[c] + weight * values[c]
                    weight = weight * (1.0 - values[3])
                for c in range(3):
                    colour[c] = colour[c] + weight * blended_ref[v, p, c, rows]
                weight = weight * blended_ref[v, p, 3, rows]
            for c in range(3):
                frame_ref[v, c, 0, rows] = colour[c]
            frame_ref[v, 3, 0, rows] = 1.0 - weight
        copies.append(pltpu.make_async_copy(frame_ref.at[v], frame_hbm.at[v], sems.at[v]))
        copies[-1].start()
    for copy in copies:
        copy.wait()


def composed_frame(blended, given):
    views, _, channels, strip, cols = blended.shape
    vmem = pl.BlockSpec(memory_space=pltpu.VMEM)
    shape = (views, channels, 1, strip, cols)
    return pl.pallas_call(
        functools.partial(frame_kernel, list(given)),
        in_specs=[vmem] * (1 + len(given)),
        out_specs=pl.BlockSpec(memory_space=pl.ANY),
        out_shape=jax.ShapeDtypeStruct(shape, jnp.float32),
        scratch_shapes=[pltpu.VMEM(shape, jnp.float32), pltpu.SemaphoreType.DMA((views,))],
        compiler_params=pltpu.CompilerParams(vmem_limit_bytes=VMEM_BYTES),
        name="compose_frame",
    )(blended, *given.values())


def on_device(density, albedo, targets, offsets, slab_order):
    depth_cells = density.shape[0]
    slabs, columns = lax.axis_size("depth"), lax.axis_size("col")
    offsets = offsets[:, :, 0, 0]
    code, density = slab_code(density)
    codes = [code] + [swap_depth(code, k, slabs) for k in range(1, slabs)]
    sums, opac = image_sums(density, albedo)
    swaps = column_swaps(slabs, columns)
    near = [swap for swap in swaps if swap[0] == 1]
    far = [swap for swap in swaps if swap[0] > 1]
    far_steps = sorted({swap[0] for swap in far})
    roles = [("near", *swap) for swap in near] + [("far", *swap) for swap in far]
    roles += [("take", step, 0, []) for step in far_steps] + [("keep", 0, 0, []), ("order", 0, 0, [])]
    masks = piece_plans(targets, offsets, slab_order, columns, sums, roles, "piece_plans")
    near_masks, masks = masks[: len(near)], masks[len(near) :]
    strips = {}
    for chosen in (list(range(1, slabs)), [0]):
        lit = lit_strips(codes, sums, opac, offsets, offsets, depth_cells, chosen)
        strips |= dict(zip(chosen, lit, strict=True))
    blocks = {0: strips[0]} | {k: swap_depth(strips[k], k, slabs) for k in range(1, slabs)}
    given = {("order",): masks[-1]}
    given |= {("take", step): mask for step, mask in zip(far_steps, masks[len(far) :], strict=False)}
    for name, chosen in (("early", tuple(range(max(1, slabs // 2)))), ("late", tuple(range(slabs - 1, max(1, slabs // 2) - 1, -1)))):
        pieces = near_pieces([blocks[k] for k in chosen], near_masks, chosen, "near_pieces_" + name)
        for (step, parity, lefts), piece in zip(near, pieces, strict=True):
            given["near", parity, chosen] = swap_columns(piece, step, lefts, slabs, columns)
    blocks = [blocks[k] for k in range(slabs)]
    if far:
        for (step, parity, lefts), piece in zip(far, packed_pieces(blocks, masks[: len(far)], "far_pieces"), strict=True):
            given["far", step, parity] = swap_columns(piece, step, lefts, slabs, columns)
    (given["own",],) = packed_pieces(blocks, masks[-2:-1], "kept_pieces")
    nears = {key: value for key, value in given.items() if key[0] in ("order", "near", "own")}
    fars = {key: value for key, value in given.items() if key not in nears}
    return composed_frame(blended_pieces(nears, slabs), fars)


def solution(mesh):
    in_specs = (
        P("depth", "row", "col"),
        P(None, "depth", "row", "col"),
        P(None, None, "row", None),
        P(None, None, "row", "col"),
        P(),
    )
    out_specs = P(None, None, "row", "depth", "col")
    return jax.shard_map(
        on_device, mesh=mesh, in_specs=in_specs, out_specs=out_specs, check_vma=False
    )
```

```python
import functools
import math

import jax
import jax.numpy as jnp
from jax import lax
from jax.experimental import pallas as pl
from jax.experimental.pallas import tpu as pltpu
from jax.sharding import PartitionSpec as P

SHEARS = (0.3125, -0.4375)
BRIGHTNESS = 4.0
DENSITY_RANGE = (0.002, 0.05)
CODE_REACH = 76.0
PAIR = 2
VMEM_BYTES = 16 * 1024 * 1024


def plane_steps(shear, depth_cells):
    whole = [math.floor(shear * z) for z in range(depth_cells)]
    return [(k, shear * z - k) for z, k in enumerate(whole)]


def column_shifts(shear, depth_cells):
    found = set()
    for k, f in plane_steps(shear, depth_cells):
        found |= {k, k + 1} if f > 0.0 else {k}
    return sorted(found)


def shift_list(depth_cells):
    return [(v, j) for v, s in enumerate(SHEARS) for j in column_shifts(s, depth_cells)]


def rolled(value, steps):
    size = value.shape[-1]
    steps = steps % size
    return pltpu.roll(value, steps, value.ndim - 1) if steps else value


def depth_code(depth_cells):
    low, high = (depth_cells * d for d in DENSITY_RANGE)
    return 0.5 * (low + high), CODE_REACH / (0.5 * (high - low))


def plane_kernel(parts, density_hbm, code_ref, density_ref, sems):
    depth_cells, rows, _ = density_ref.shape
    block = rows // parts
    middle, spread = depth_code(depth_cells)
    copies = []
    for i in range(parts):
        part = pl.ds(i * block, block)
        copies.append(pltpu.make_async_copy(density_hbm.at[:, part], density_ref.at[:, part], sems.at[i]))
    for copy in copies:
        copy.start()
    for i in range(parts):
        copies[i].wait()
        part = pl.ds(i * block, block)
        total = density_ref[0, part]
        for z in range(1, depth_cells):
            total = total + density_ref[z, part]
        code = jnp.exp(jnp.clip((total - middle) * spread, -CODE_REACH, CODE_REACH))
        code_ref[part] = code.astype(jnp.bfloat16)


def slab_code(density):
    parts = max(1, density.shape[1] // 32)
    return pl.pallas_call(
        functools.partial(plane_kernel, parts),
        in_specs=[pl.BlockSpec(memory_space=pl.ANY)],
        out_specs=[pl.BlockSpec(memory_space=pltpu.VMEM)] * 2,
        out_shape=[
            pltpu.VMEM(density.shape[1:], jnp.bfloat16),
            pltpu.VMEM(density.shape, density.dtype),
        ],
        scratch_shapes=[pltpu.SemaphoreType.DMA((parts,))],
        compiler_params=pltpu.CompilerParams(vmem_limit_bytes=VMEM_BYTES),
        name="slab_code",
    )(pltpu.with_memory_space_constraint(density, pltpu.HBM))


def opacity_weights(k, f, lane, cols):
    if k >= 0:
        inside = lane < cols - k
        return (jnp.where(inside, 1.0 - f, 0.0), jnp.where(inside & (lane >= 1), f, 0.0))
    inside = lane >= -k
    return (jnp.where(inside, 1.0 - f, 0.0), jnp.where(inside | (lane == 0), f, 0.0))


def share_list(depth_cells):
    found = []
    for v, shear in enumerate(SHEARS):
        for z, (k, f) in enumerate(plane_steps(shear, depth_cells)):
            found += [(v, z, j, share) for j, share in ((k, 1.0 - f), (k + 1, f)) if share > 0.0]
    return found


def weigh_rows(density_ref, weights_ref, opac_ref, rows):
    depth_cells, _, cols = density_ref.shape
    tiled = (rows.size // 8, 8, cols)
    lane = lax.broadcasted_iota(jnp.int32, (8, cols), 1)
    shares = share_list(depth_cells)
    steps = [plane_steps(s, depth_cells) for s in SHEARS]
    transmit = [jnp.ones(tiled, jnp.float32) for _ in SHEARS]
    frame = [0 for _ in SHEARS]
    light = jnp.full(tiled, BRIGHTNESS, jnp.float32)
    for z in range(depth_cells):
        kept = jnp.exp(-density_ref[z, rows].reshape(tiled))
        opacity = 1.0 - kept
        lit = light * opacity
        light = light * kept
        farther = rolled(opacity, 1)
        for v in range(len(SHEARS)):
            k, f = steps[v][z]
            transmit[v] = rolled(transmit[v], frame[v] - k)
            frame[v] = k
            for i, (view, plane, j, share) in enumerate(shares):
                if (view, plane) == (v, z):
                    here = transmit[v] if j == k else rolled(transmit[v], -1)
                    weights_ref[i, rows] = (here * (lit * share)).reshape(rows.size, cols)
            a, b = opacity_weights(k, f, lane, cols)
            moved = a[None] * opacity if f == 0.0 else a[None] * opacity + b[None] * farther
            transmit[v] = transmit[v] * (1.0 - moved)
    for v in range(len(SHEARS)):
        opac_ref[v, rows] = (1.0 - rolled(transmit[v], frame[v])).reshape(rows.size, cols).astype(opac_ref.dtype)


def sum_rows(albedo_ref, weights_ref, sums_ref, rows):
    _, depth_cells, _, cols = albedo_ref.shape
    lane = lax.broadcasted_iota(jnp.int32, (8, cols), 1)
    shares = share_list(depth_cells)
    index = {key: i for i, key in enumerate(shift_list(depth_cells))}
    last = {(v, j): z for v, z, j, _ in shares}
    sums = {}
    for z in range(depth_cells):
        colour = [albedo_ref[c, z, rows].astype(jnp.float32) for c in range(3)]
        for i, (v, plane, j, _) in enumerate(shares):
            if plane != z:
                continue
            weight = weights_ref[i, rows]
            for c in range(3):
                term = weight * colour[c]
                total = sums.pop((v, j, c)) + term if (v, j, c) in sums else term
                if last[v, j] > z:
                    sums[v, j, c] = total
                    continue
                if j:
                    inside = lane < cols - j if j > 0 else lane >= -j
                    total = jnp.where(inside[None], total.reshape(-1, 8, cols), 0.0).reshape(total.shape)
                sums_ref[index[v, j] * 3 + c, rows] = total


def sums_kernel(
    chunk, block, density_ref, albedo_hbm, sums_ref, opac_ref, weights_ref, albedo_ref, sems
):
    count = density_ref.shape[1]
    parts = sems.shape[0]

    def copy(i):
        part = pl.ds(i * (count // parts), count // parts)
        return pltpu.make_async_copy(albedo_hbm.at[:, :, part], albedo_ref.at[:, :, part], sems.at[i])

    for i in range(parts):
        copy(i).start()

    def weigh(i, carry):
        weigh_rows(density_ref, weights_ref, opac_ref, pl.ds(pl.multiple_of(i * block, block), block))
        return carry

    def add(i, carry):
        sum_rows(albedo_ref, weights_ref, sums_ref, pl.ds(pl.multiple_of(i * chunk, chunk), chunk))
        return carry

    lax.fori_loop(0, count // block, weigh, 0)
    for i in range(parts):
        copy(i).wait()
    lax.fori_loop(0, count // chunk, add, 0)


def image_sums(density, albedo):
    depth_cells, rows, cols = density.shape
    count = 3 * len(shift_list(depth_cells))
    cells = depth_cells * rows * cols
    vmem = pl.BlockSpec(memory_space=pltpu.VMEM)
    return pl.pallas_call(
        functools.partial(sums_kernel, 16, min(rows, 128)),
        in_specs=[vmem, pl.BlockSpec(memory_space=pl.ANY)],
        out_specs=[vmem, vmem],
        out_shape=[
            pltpu.VMEM((count, rows, cols), jnp.float32),
            pltpu.VMEM((len(SHEARS), rows, cols), jnp.bfloat16),
        ],
        scratch_shapes=[
            pltpu.VMEM((len(share_list(depth_cells)), rows, cols), jnp.float32),
            pltpu.VMEM(albedo.shape, albedo.dtype),
            pltpu.SemaphoreType.DMA((max(1, rows // 32),)),
        ],
        compiler_params=pltpu.CompilerParams(vmem_limit_bytes=VMEM_BYTES),
        cost_estimate=pl.CostEstimate(
            flops=60 * cells, bytes_accessed=10 * cells + 4 * count * rows * cols, transcendentals=cells
        ),
        name="image_sums",
    )(density, pltpu.with_memory_space_constraint(albedo, pltpu.HBM))


def partner(mine, k, count):
    return mine ^ k if count & (count - 1) == 0 else lax.rem(mine + k, count)


def origin(mine, k, count):
    return mine ^ k if count & (count - 1) == 0 else lax.rem(mine - k + count, count)


def swap_depth(value, k, count):
    return lax.ppermute(value, "depth", [(i, int(partner(i, k, count)) if count & (count - 1) == 0 else (i + k) % count) for i in range(count)])


def turn_matrix(offsets, view, slab, cols):
    lane = lax.broadcasted_iota(jnp.int32, offsets.shape, 1)
    row = lax.broadcasted_iota(jnp.int32, offsets.shape, 0)
    own = jnp.where((lane == slab) & (row == view), offsets, 0).astype(jnp.float32)
    offset = jnp.sum(jnp.sum(own, axis=1, keepdims=True), axis=0, keepdims=True).astype(jnp.int32)
    moved = lax.broadcasted_iota(jnp.int32, (cols, cols), 0) + offset
    moved = jnp.where(moved >= cols, moved - cols, moved)
    landing = lax.broadcasted_iota(jnp.int32, (cols, cols), 1)
    return (moved == landing).astype(jnp.float32).astype(jnp.bfloat16)


def lit_kernel(slabs, depth_cells, chosen, offsets_ref, after_ref, *refs):
    codes, (sums_ref, opac_ref), outs = refs[:slabs], refs[slabs : slabs + 2], refs[slabs + 2 :]
    codes = [codes[-k % slabs] for k in range(slabs)]
    mine = lax.axis_index("depth")
    strip, cols = outs[0].shape[2:]
    keys = shift_list(depth_cells)
    middle, spread = depth_code(depth_cells)
    turns = [turn_matrix(offsets_ref[...], v, mine, cols) for v in range(len(SHEARS))]
    for k, out in zip(chosen, outs, strict=True):
        rows = pl.ds(pl.multiple_of(partner(mine, k, slabs) * strip, strip), strip)
        ahead_depth = jnp.zeros((strip, cols), jnp.float32)
        for other in range(1, slabs):
            ahead = origin(mine, other, slabs) < mine
            depth = jnp.log(codes[other][rows].astype(jnp.float32)) * (1.0 / spread) + middle
            ahead_depth = ahead_depth + jnp.where(ahead, depth, 0.0)
        incoming = jnp.exp(-ahead_depth)
        for v in range(len(SHEARS)):
            image = []
            for c in range(3):
                total = None
                for i, (view, j) in enumerate(keys):
                    if view != v:
                        continue
                    moved = rolled(incoming * sums_ref[i * 3 + c, rows], j)
                    total = moved if total is None else total + moved
                image.append(total.astype(jnp.bfloat16))
            image = jnp.concatenate([*image, opac_ref[v, rows]], axis=0)
            turned = jnp.dot(image, turns[v], preferred_element_type=jnp.float32)
            out[v] = turned.astype(jnp.bfloat16).reshape(4, strip, cols)


def lit_strips(codes, sums, opac, offsets, after, depth_cells, chosen):
    slabs = len(codes)
    rows, cols = codes[0].shape
    strip = rows // slabs
    vmem = pl.BlockSpec(memory_space=pltpu.VMEM)
    return pl.pallas_call(
        functools.partial(lit_kernel, slabs, depth_cells, chosen),
        in_specs=[vmem, pl.BlockSpec(memory_space=pl.ANY)] + [vmem] * (slabs + 2),
        out_specs=[vmem] * len(chosen),
        out_shape=[jax.ShapeDtypeStruct((len(SHEARS), 4, strip, cols), jnp.bfloat16)] * len(chosen),
        compiler_params=pltpu.CompilerParams(vmem_limit_bytes=VMEM_BYTES),
        name="lit_strips_" + "".join(str(k) for k in chosen),
    )(offsets, after, *[codes[-k % slabs] for k in range(slabs)], sums, opac)


def piece_slots(step, slabs):
    return min(slabs, 2 * PAIR if step < slabs // 2 else PAIR)


def column_swaps(slabs, columns):
    swaps = []
    for step in range(1, slabs // 2 + 1):
        for parity in range(2):
            lefts = [c for c in range(columns - step) if (c // step) % 2 == parity]
            if step > 1 and step == slabs // 2:
                lefts = [c for c in lefts if c > 0]
            if lefts:
                swaps.append((step, parity, lefts))
    return swaps


def swap_columns(value, step, lefts, slabs, columns):
    to = {c: c + step for c in lefts} | {c + step: c for c in lefts}
    rows = lax.axis_size("row")
    pairs = []
    for d in range(slabs):
        for r in range(rows):
            for c in range(columns):
                way = 0 if step == 1 else 0
                there = (d, r, to[c]) if c in to else ((d, r ^ 1, c) if way == 0 else (d ^ way, r, c))
                if there[0] < slabs and there[1] < rows:
                    pairs.append(((d * rows + r) * columns + c, (there[0] * rows + there[1]) * columns + there[2]))
    return lax.ppermute(value, ("depth", "row", "col"), pairs)


def covers(targets_ref, view, slab, column, tile):
    first = targets_ref[view, slab, 0, column]
    return (first == tile) | (first + 1 == tile)


def plan_kernel(slabs, columns, plans, targets_ref, offsets_ref, order_ref, *refs):
    outs = refs[1:]
    mine, column = lax.axis_index("depth"), lax.axis_index("col")
    cols = outs[0].shape[-1]
    shape = (8, cols)
    lane = lax.broadcasted_iota(jnp.int32, shape, 1).astype(jnp.float32)

    def pick(table, row, at):
        rows = lax.broadcasted_iota(jnp.int32, table.shape, 0)
        lanes = lax.broadcasted_iota(jnp.int32, table.shape, 1)
        entry = jnp.where((rows == row) & (lanes == at), table, 0).astype(jnp.float32)
        return jnp.broadcast_to(jnp.sum(jnp.sum(entry, axis=1, keepdims=True), axis=0, keepdims=True), shape)

    def flag(condition):
        return jnp.where(condition, 1.0, 0.0)

    def put(out, at, value):
        out[at] = jnp.concatenate([value, value], axis=0).astype(out.dtype)

    def same(scalar):
        return jnp.full(shape, scalar, jnp.int32).astype(jnp.float32)

    for v in range(len(SHEARS)):
        targets = targets_ref[v, :, 0, :]
        order = [pick(order_ref[...], v, p) for p in range(slabs)]
        slab = [same(origin(mine, k, slabs)) for k in range(slabs)]
        first = [pick(targets, origin(mine, k, slabs), column) for k in range(slabs)]
        offset = [pick(offsets_ref[...], v, origin(mine, k, slabs)) for k in range(slabs)]
        places = [[flag(order[p] == slab[k]) for k in range(slabs)] for p in range(slabs)]

        def columns_of(k, tile):
            return jnp.where(lane >= offset[k], flag(first[k] == tile), flag(first[k] + 1.0 == tile))

        def found_before(firsts, slabs_there, tile):
            count, found = jnp.zeros(shape, jnp.float32), []
            for p in range(slabs):
                here = jnp.zeros(shape, jnp.float32)
                for start, number in zip(firsts, slabs_there, strict=True):
                    covered = flag(start == tile) + flag(start + 1.0 == tile)
                    here = here + flag(order[p] == number) * covered
                found.append((here, count))
                count = count + here
            return found

        for out, (role, step, parity, lefts) in zip(outs, plans, strict=True):
            tile = same(column)
            if role in ("near", "far"):
                is_left = lax.rem(lax.div(column, step), 2) == parity
                is_left = is_left & (column >= lefts[0]) & (column + step < columns)
                is_right = (lax.rem(column, 2) != parity) & (column - step >= lefts[0]) & (step == 1)
                tile = same(jnp.where(is_left, column + step, jnp.where(is_right, column - step, -PAIR)))
            if role == "near":
                for k in range(slabs):
                    put(out, (v, k), columns_of(k, tile))
            elif role == "keep":
                own = [columns_of(k, tile) for k in range(slabs)]
                for p in range(slabs):
                    for k in range(slabs):
                        put(out, (v, p, k), places[p][k] * own[k])
            elif role == "order":
                for p in range(slabs):
                    for k in range(slabs):
                        put(out, (v, p, k), places[p][k])
            elif role == "far":
                found = found_before(first, slab, tile)
                there = [columns_of(k, tile) for k in range(slabs)]
                for slot in range(out.shape[1]):
                    chosen = [here * flag(count == slot) for here, count in found]
                    for k in range(slabs):
                        fits = chosen[0] * places[0][k]
                        for p in range(1, slabs):
                            fits = fits + chosen[p] * places[p][k]
                        put(out, (v, slot, k), fits * there[k])
            elif role == "take":
                source = column - step
                present = same(((source >= 0) & (source < columns)).astype(jnp.int32))
                firsts = [pick(targets, d, source) for d in range(slabs)]
                numbers = [same(d) for d in range(slabs)]
                for p, (here, count) in enumerate(found_before(firsts, numbers, tile)):
                    for slot in range(out.shape[2]):
                        put(out, (v, p, slot), here * present * flag(count == slot))


def piece_plans(targets, offsets, slab_order, columns, after, plans, name):
    slabs = slab_order.shape[1]
    views, cols = len(SHEARS), after.shape[-1]
    vmem = pl.BlockSpec(memory_space=pltpu.VMEM)
    shapes = {"near": lambda n: (slabs,), "far": lambda n: (n, slabs), "take": lambda n: (slabs, n)}
    shapes = [shapes.get(role, lambda n: (slabs, slabs))(piece_slots(step, slabs)) for role, step, _, _ in plans]
    return pl.pallas_call(
        functools.partial(plan_kernel, slabs, columns, plans),
        in_specs=[vmem] * 4,
        out_specs=[vmem] * len(plans),
        out_shape=[pltpu.VMEM((views, *shape, 16, cols), jnp.bfloat16) for shape in shapes],
        compiler_params=pltpu.CompilerParams(vmem_limit_bytes=VMEM_BYTES),
        name=name,
    )(targets, offsets, slab_order, after)


def near_kernel(chosen, outs_count, *refs):
    blocks, masks, outs = refs[: len(chosen)], refs[len(chosen) : -outs_count - 1], refs[-outs_count:]
    for mask_ref, out in zip(masks, outs, strict=True):
        views, _, channels, strip, _ = out.shape
        for v in range(views):
            for i, k in enumerate(chosen):
                mask = mask_ref[v, k]
                for c in range(channels):
                    for row in range(0, strip, 16):
                        rows = pl.ds(row, 16)
                        out[v, i, c, rows] = blocks[i][v, c, rows] * mask


def near_pieces(blocks, masks, chosen, name, after):
    views, channels, strip, cols = blocks[0].shape
    vmem = pl.BlockSpec(memory_space=pltpu.VMEM)
    return pl.pallas_call(
        functools.partial(near_kernel, chosen, len(masks)),
        in_specs=[vmem] * (len(blocks) + len(masks)) + [pl.BlockSpec(memory_space=pl.ANY)],
        out_specs=[vmem] * len(masks),
        out_shape=[jax.ShapeDtypeStruct((views, len(chosen), channels, strip, cols), jnp.bfloat16) for _ in masks],
        compiler_params=pltpu.CompilerParams(vmem_limit_bytes=VMEM_BYTES),
        name=name,
    )(*blocks, *masks, after)


def pack_kernel(slabs, outs_count, *refs):
    blocks, masks, outs = refs[:slabs], refs[slabs : slabs + outs_count], refs[slabs + outs_count :]
    for mask_ref, out in zip(masks, outs, strict=True):
        views, slots, channels, strip, _ = out.shape
        for v in range(views):
            for slot in range(slots):
                parts = [mask_ref[v, slot, k] for k in range(slabs)]
                for row in range(0, strip, 16):
                    rows = pl.ds(row, 16)
                    for c in range(channels):
                        total = blocks[0][v, c, rows] * parts[0]
                        for k in range(1, slabs):
                            total = total + blocks[k][v, c, rows] * parts[k]
                        out[v, slot, c, rows] = total


def packed_pieces(blocks, masks, name):
    slabs = len(blocks)
    views, channels, strip, cols = blocks[0].shape
    vmem = pl.BlockSpec(memory_space=pltpu.VMEM)
    return pl.pallas_call(
        functools.partial(pack_kernel, slabs, len(masks)),
        in_specs=[vmem] * (slabs + len(masks)),
        out_specs=[vmem] * len(masks),
        out_shape=[
            jax.ShapeDtypeStruct((views, mask.shape[1], channels, strip, cols), jnp.bfloat16) for mask in masks
        ],
        compiler_params=pltpu.CompilerParams(vmem_limit_bytes=VMEM_BYTES),
        name=name,
    )(*blocks, *masks)


def blend_kernel(names, *refs):
    given, out = dict(zip(names, refs[:-1], strict=True)), refs[-1]
    views, slabs, _, strip, cols = out.shape
    order_ref = given["order",]
    tile = lax.axis_index("col")
    near = {parity: [] for parity in range(2)}
    for (kind, *key), ref in given.items():
        if kind == "near":
            near[key[0]].append((key[1], ref))

    def by_strip(groups, v, p, c, rows):
        total = None
        for chosen, ref in groups:
            for i, k in enumerate(chosen):
                term = ref[v, i, c, rows] * order_ref[v, p, k]
                total = term if total is None else total + term
        return total

    def blend(left, right):
        for v in range(views):
            for p in range(slabs):
                for row in range(0, strip, 16):
                    rows = pl.ds(row, 16)
                    colour = [jnp.zeros((16, cols), jnp.float32) for _ in range(3)]
                    through = jnp.ones((16, cols), jnp.float32)
                    for source in (left, None, right):
                        if source is None:
                            values = [given["own",][v, p, c, rows] for c in range(4)]
                        elif source:
                            values = [by_strip(source, v, p, c, rows) for c in range(4)]
                        else:
                            continue
                        values = [value.astype(jnp.float32) for value in values]
                        for c in range(3):
                            colour[c] = colour[c] + through * values[c]
                        through = through * (1.0 - values[3])
                    for c in range(3):
                        out[v, p, c, rows] = colour[c]
                    out[v, p, 3, rows] = through

    for phase in range(2):
        pl.when(lax.rem(tile, 2) == phase)(functools.partial(blend, near[(phase - 1) % 2], near[phase]))


def blended_pieces(given, slabs):
    views, _, channels, strip, cols = given["own",].shape
    vmem = pl.BlockSpec(memory_space=pltpu.VMEM)
    return pl.pallas_call(
        functools.partial(blend_kernel, list(given)),
        in_specs=[vmem] * len(given),
        out_specs=vmem,
        out_shape=pltpu.VMEM((views, slabs, channels, strip, cols), jnp.float32),
        compiler_params=pltpu.CompilerParams(vmem_limit_bytes=VMEM_BYTES),
        name="blend_pieces",
    )(*given.values())


def frame_kernel(names, *refs):
    blended_ref, given = refs[0], dict(zip(names, refs[1:-3], strict=True))
    frame_hbm, frame_ref, sems = refs[-3:]
    views, slabs, _, strip, cols = blended_ref.shape
    tile = lax.axis_index("col")
    steps = sorted({key[1] for key in given if key[0] == "take"}, reverse=True)

    def placed(step, v, p, c, rows):
        arrived = [given["far", step, q] for q in range(2) if ("far", step, q) in given]
        pieces = []
        for ref in arrived:
            total = ref[v, 0, c, rows] * given["take", step][v, p, 0]
            for slot in range(1, ref.shape[1]):
                total = total + ref[v, slot, c, rows] * given["take", step][v, p, slot]
            pieces.append(total)
        first = lax.rem(lax.div(tile + step, step), 2) == 0
        return pieces[0] if len(pieces) == 1 else jnp.where(first, pieces[0], pieces[1])

    copies = []
    for v in range(views):
        for row in range(0, strip, 16):
            rows = pl.ds(row, 16)
            colour = [jnp.zeros((16, cols), jnp.float32) for _ in range(3)]
            weight = jnp.ones((16, cols), jnp.float32)
            for p in range(slabs):
                for step in steps:
                    values = [placed(step, v, p, c, rows).astype(jnp.float32) for c in range(4)]
                    for c in range(3):
                        colour[c] = colour[c] + weight * values[c]
                    weight = weight * (1.0 - values[3])
                for c in range(3):
                    colour[c] = colour[c] + weight * blended_ref[v, p, c, rows]
                weight = weight * blended_ref[v, p, 3, rows]
            for c in range(3):
                frame_ref[v, c, 0, rows] = colour[c]
            frame_ref[v, 3, 0, rows] = 1.0 - weight
        copies.append(pltpu.make_async_copy(frame_ref.at[v], frame_hbm.at[v], sems.at[v]))
        copies[-1].start()
    for copy in copies:
        copy.wait()


def composed_frame(blended, given):
    views, _, channels, strip, cols = blended.shape
    vmem = pl.BlockSpec(memory_space=pltpu.VMEM)
    shape = (views, channels, 1, strip, cols)
    return pl.pallas_call(
        functools.partial(frame_kernel, list(given)),
        in_specs=[vmem] * (1 + len(given)),
        out_specs=pl.BlockSpec(memory_space=pl.ANY),
        out_shape=jax.ShapeDtypeStruct(shape, jnp.float32),
        scratch_shapes=[pltpu.VMEM(shape, jnp.float32), pltpu.SemaphoreType.DMA((views,))],
        compiler_params=pltpu.CompilerParams(vmem_limit_bytes=VMEM_BYTES),
        name="compose_frame",
    )(blended, *given.values())


def on_device(density, albedo, targets, offsets, slab_order):
    depth_cells = density.shape[0]
    slabs, columns = lax.axis_size("depth"), lax.axis_size("col")
    offsets = offsets[:, :, 0, 0]
    code, density = slab_code(density)
    codes = [code] + [swap_depth(code, k, slabs) for k in range(1, slabs)]
    sums, opac = image_sums(density, albedo)
    swaps = column_swaps(slabs, columns)
    near = [swap for swap in swaps if swap[0] == 1]
    far = [swap for swap in swaps if swap[0] > 1]
    far_steps = sorted({swap[0] for swap in far})
    roles = [("near", *swap) for swap in near] + [("far", *swap) for swap in far]
    roles += [("take", step, 0, []) for step in far_steps] + [("keep", 0, 0, []), ("order", 0, 0, [])]
    masks = piece_plans(targets, offsets, slab_order, columns, sums, roles, "piece_plans")
    near_masks, masks = masks[: len(near)], masks[len(near) :]
    strips = {}
    for chosen in (list(range(1, slabs)), [0]):
        lit = lit_strips(codes, sums, opac, offsets, offsets, depth_cells, chosen)
        strips |= dict(zip(chosen, lit, strict=True))
    blocks = {0: strips[0]} | {k: swap_depth(strips[k], k, slabs) for k in range(1, slabs)}
    given = {("order",): masks[-1]}
    given |= {("take", step): mask for step, mask in zip(far_steps, masks[len(far) :], strict=False)}
    after = strips[0]
    for name, chosen in (("early", tuple(range(max(1, slabs // 2)))), ("late", tuple(range(slabs - 1, max(1, slabs // 2) - 1, -1)))):
        if name == "late" and far:
            for (step, parity, lefts), piece in zip(far, packed_pieces([blocks[k] for k in range(slabs)], masks[: len(far)], "far_pieces"), strict=True):
                given["far", step, parity] = swap_columns(piece, step, lefts, slabs, columns)
                after = piece
        pieces = near_pieces([blocks[k] for k in chosen], near_masks, chosen, "near_pieces_" + name, after)
        for (step, parity, lefts), piece in zip(near, pieces, strict=True):
            given["near", parity, chosen] = swap_columns(piece, step, lefts, slabs, columns)
    blocks = [blocks[k] for k in range(slabs)]
    (given["own",],) = packed_pieces(blocks, masks[-2:-1], "kept_pieces")
    nears = {key: value for key, value in given.items() if key[0] in ("order", "near", "own")}
    fars = {key: value for key, value in given.items() if key not in nears}
    return composed_frame(blended_pieces(nears, slabs), fars)


def solution(mesh):
    in_specs = (
        P("depth", "row", "col"),
        P(None, "depth", "row", "col"),
        P(None, None, "row", None),
        P(None, None, "row", "col"),
        P(),
    )
    out_specs = P(None, None, "row", "depth", "col")
    return jax.shard_map(
        on_device, mesh=mesh, in_specs=in_specs, out_specs=out_specs, check_vma=False
    )
```

```python
import functools
import math

import jax
import jax.numpy as jnp
from jax import lax
from jax.experimental import pallas as pl
from jax.experimental.pallas import tpu as pltpu
from jax.sharding import PartitionSpec as P

SHEARS = (0.3125, -0.4375)
BRIGHTNESS = 4.0
DENSITY_RANGE = (0.002, 0.05)
CODE_REACH = 76.0
PAIR = 2
VMEM_BYTES = 16 * 1024 * 1024


def plane_steps(shear, depth_cells):
    whole = [math.floor(shear * z) for z in range(depth_cells)]
    return [(k, shear * z - k) for z, k in enumerate(whole)]


def column_shifts(shear, depth_cells):
    found = set()
    for k, f in plane_steps(shear, depth_cells):
        found |= {k, k + 1} if f > 0.0 else {k}
    return sorted(found)


def shift_list(depth_cells):
    return [(v, j) for v, s in enumerate(SHEARS) for j in column_shifts(s, depth_cells)]


def rolled(value, steps):
    size = value.shape[-1]
    steps = steps % size
    return pltpu.roll(value, steps, value.ndim - 1) if steps else value


def depth_code(depth_cells):
    low, high = (depth_cells * d for d in DENSITY_RANGE)
    return 0.5 * (low + high), CODE_REACH / (0.5 * (high - low))


def plane_kernel(parts, density_hbm, code_ref, density_ref, sems):
    depth_cells, rows, _ = density_ref.shape
    block = rows // parts
    middle, spread = depth_code(depth_cells)
    copies = []
    for i in range(parts):
        part = pl.ds(i * block, block)
        copies.append(pltpu.make_async_copy(density_hbm.at[:, part], density_ref.at[:, part], sems.at[i]))
    for copy in copies:
        copy.start()
    for i in range(parts):
        copies[i].wait()
        part = pl.ds(i * block, block)
        total = density_ref[0, part]
        for z in range(1, depth_cells):
            total = total + density_ref[z, part]
        code = jnp.exp(jnp.clip((total - middle) * spread, -CODE_REACH, CODE_REACH))
        code_ref[part] = code.astype(jnp.bfloat16)


def slab_code(density):
    parts = max(1, density.shape[1] // 32)
    return pl.pallas_call(
        functools.partial(plane_kernel, parts),
        in_specs=[pl.BlockSpec(memory_space=pl.ANY)],
        out_specs=[pl.BlockSpec(memory_space=pltpu.VMEM)] * 2,
        out_shape=[
            pltpu.VMEM(density.shape[1:], jnp.bfloat16),
            pltpu.VMEM(density.shape, density.dtype),
        ],
        scratch_shapes=[pltpu.SemaphoreType.DMA((parts,))],
        compiler_params=pltpu.CompilerParams(vmem_limit_bytes=VMEM_BYTES),
        name="slab_code",
    )(pltpu.with_memory_space_constraint(density, pltpu.HBM))


def opacity_weights(k, f, lane, cols):
    if k >= 0:
        inside = lane < cols - k
        return (jnp.where(inside, 1.0 - f, 0.0), jnp.where(inside & (lane >= 1), f, 0.0))
    inside = lane >= -k
    return (jnp.where(inside, 1.0 - f, 0.0), jnp.where(inside | (lane == 0), f, 0.0))


def share_list(depth_cells):
    found = []
    for v, shear in enumerate(SHEARS):
        for z, (k, f) in enumerate(plane_steps(shear, depth_cells)):
            found += [(v, z, j, share) for j, share in ((k, 1.0 - f), (k + 1, f)) if share > 0.0]
    return found


def weigh_rows(density_ref, weights_ref, opac_ref, rows):
    depth_cells, _, cols = density_ref.shape
    tiled = (rows.size // 8, 8, cols)
    lane = lax.broadcasted_iota(jnp.int32, (8, cols), 1)
    shares = share_list(depth_cells)
    steps = [plane_steps(s, depth_cells) for s in SHEARS]
    transmit = [jnp.ones(tiled, jnp.float32) for _ in SHEARS]
    frame = [0 for _ in SHEARS]
    light = jnp.full(tiled, BRIGHTNESS, jnp.float32)
    for z in range(depth_cells):
        kept = jnp.exp(-density_ref[z, rows].reshape(tiled))
        opacity = 1.0 - kept
        lit = light * opacity
        light = light * kept
        farther = rolled(opacity, 1)
        for v in range(len(SHEARS)):
            k, f = steps[v][z]
            transmit[v] = rolled(transmit[v], frame[v] - k)
            frame[v] = k
            for i, (view, plane, j, share) in enumerate(shares):
                if (view, plane) == (v, z):
                    here = transmit[v] if j == k else rolled(transmit[v], -1)
                    weights_ref[i, rows] = (here * (lit * share)).reshape(rows.size, cols)
            a, b = opacity_weights(k, f, lane, cols)
            moved = a[None] * opacity if f == 0.0 else a[None] * opacity + b[None] * farther
            transmit[v] = transmit[v] * (1.0 - moved)
    for v in range(len(SHEARS)):
        opac_ref[v, rows] = (1.0 - rolled(transmit[v], frame[v])).reshape(rows.size, cols).astype(opac_ref.dtype)


def sum_rows(albedo_ref, weights_ref, sums_ref, rows):
    _, depth_cells, _, cols = albedo_ref.shape
    lane = lax.broadcasted_iota(jnp.int32, (8, cols), 1)
    shares = share_list(depth_cells)
    index = {key: i for i, key in enumerate(shift_list(depth_cells))}
    last = {(v, j): z for v, z, j, _ in shares}
    sums = {}
    for z in range(depth_cells):
        colour = [albedo_ref[c, z, rows].astype(jnp.float32) for c in range(3)]
        for i, (v, plane, j, _) in enumerate(shares):
            if plane != z:
                continue
            weight = weights_ref[i, rows]
            for c in range(3):
                term = weight * colour[c]
                total = sums.pop((v, j, c)) + term if (v, j, c) in sums else term
                if last[v, j] > z:
                    sums[v, j, c] = total
                    continue
                if j:
                    inside = lane < cols - j if j > 0 else lane >= -j
                    total = jnp.where(inside[None], total.reshape(-1, 8, cols), 0.0).reshape(total.shape)
                sums_ref[index[v, j] * 3 + c, rows] = total


def sums_kernel(
    chunk, block, density_ref, albedo_hbm, sums_ref, opac_ref, weights_ref, albedo_ref, sems
):
    count = density_ref.shape[1]
    parts = sems.shape[0]

    def copy(i):
        part = pl.ds(i * (count // parts), count // parts)
        return pltpu.make_async_copy(albedo_hbm.at[:, :, part], albedo_ref.at[:, :, part], sems.at[i])

    for i in range(parts):
        copy(i).start()

    def weigh(i, carry):
        weigh_rows(density_ref, weights_ref, opac_ref, pl.ds(pl.multiple_of(i * block, block), block))
        return carry

    def add(i, carry):
        sum_rows(albedo_ref, weights_ref, sums_ref, pl.ds(pl.multiple_of(i * chunk, chunk), chunk))
        return carry

    lax.fori_loop(0, count // block, weigh, 0)
    for i in range(parts):
        copy(i).wait()
    lax.fori_loop(0, count // chunk, add, 0)


def image_sums(density, albedo):
    depth_cells, rows, cols = density.shape
    count = 3 * len(shift_list(depth_cells))
    cells = depth_cells * rows * cols
    vmem = pl.BlockSpec(memory_space=pltpu.VMEM)
    return pl.pallas_call(
        functools.partial(sums_kernel, 16, min(rows, 128)),
        in_specs=[vmem, pl.BlockSpec(memory_space=pl.ANY)],
        out_specs=[vmem, vmem],
        out_shape=[
            pltpu.VMEM((count, rows, cols), jnp.float32),
            pltpu.VMEM((len(SHEARS), rows, cols), jnp.bfloat16),
        ],
        scratch_shapes=[
            pltpu.VMEM((len(share_list(depth_cells)), rows, cols), jnp.float32),
            pltpu.VMEM(albedo.shape, albedo.dtype),
            pltpu.SemaphoreType.DMA((max(1, rows // 32),)),
        ],
        compiler_params=pltpu.CompilerParams(vmem_limit_bytes=VMEM_BYTES),
        cost_estimate=pl.CostEstimate(
            flops=60 * cells, bytes_accessed=10 * cells + 4 * count * rows * cols, transcendentals=cells
        ),
        name="image_sums",
    )(density, pltpu.with_memory_space_constraint(albedo, pltpu.HBM))


def partner(mine, k, count):
    return mine ^ k if count & (count - 1) == 0 else lax.rem(mine + k, count)


def origin(mine, k, count):
    return mine ^ k if count & (count - 1) == 0 else lax.rem(mine - k + count, count)


def swap_depth(value, k, count):
    return lax.ppermute(value, "depth", [(i, int(partner(i, k, count)) if count & (count - 1) == 0 else (i + k) % count) for i in range(count)])


def turn_matrix(offsets, view, slab, cols):
    lane = lax.broadcasted_iota(jnp.int32, offsets.shape, 1)
    row = lax.broadcasted_iota(jnp.int32, offsets.shape, 0)
    own = jnp.where((lane == slab) & (row == view), offsets, 0).astype(jnp.float32)
    offset = jnp.sum(jnp.sum(own, axis=1, keepdims=True), axis=0, keepdims=True).astype(jnp.int32)
    moved = lax.broadcasted_iota(jnp.int32, (cols, cols), 0) + offset
    moved = jnp.where(moved >= cols, moved - cols, moved)
    landing = lax.broadcasted_iota(jnp.int32, (cols, cols), 1)
    return (moved == landing).astype(jnp.float32).astype(jnp.bfloat16)


def lit_kernel(slabs, depth_cells, chosen, offsets_ref, after_ref, *refs):
    codes, (sums_ref, opac_ref), outs = refs[:slabs], refs[slabs : slabs + 2], refs[slabs + 2 :]
    codes = [codes[-k % slabs] for k in range(slabs)]
    mine = lax.axis_index("depth")
    strip, cols = outs[0].shape[2:]
    keys = shift_list(depth_cells)
    middle, spread = depth_code(depth_cells)
    turns = [turn_matrix(offsets_ref[...], v, mine, cols) for v in range(len(SHEARS))]
    for k, out in zip(chosen, outs, strict=True):
        rows = pl.ds(pl.multiple_of(partner(mine, k, slabs) * strip, strip), strip)
        ahead_depth = jnp.zeros((strip, cols), jnp.float32)
        for other in range(1, slabs):
            ahead = origin(mine, other, slabs) < mine
            depth = jnp.log(codes[other][rows].astype(jnp.float32)) * (1.0 / spread) + middle
            ahead_depth = ahead_depth + jnp.where(ahead, depth, 0.0)
        incoming = jnp.exp(-ahead_depth)
        for v in range(len(SHEARS)):
            image = []
            for c in range(3):
                total = None
                for i, (view, j) in enumerate(keys):
                    if view != v:
                        continue
                    moved = rolled(incoming * sums_ref[i * 3 + c, rows], j)
                    total = moved if total is None else total + moved
                image.append(total.astype(jnp.bfloat16))
            image = jnp.concatenate([*image, opac_ref[v, rows]], axis=0)
            turned = jnp.dot(image, turns[v], preferred_element_type=jnp.float32)
            out[v] = turned.astype(jnp.bfloat16).reshape(4, strip, cols)


def lit_strips(codes, sums, opac, offsets, after, depth_cells, chosen):
    slabs = len(codes)
    rows, cols = codes[0].shape
    strip = rows // slabs
    vmem = pl.BlockSpec(memory_space=pltpu.VMEM)
    return pl.pallas_call(
        functools.partial(lit_kernel, slabs, depth_cells, chosen),
        in_specs=[vmem, pl.BlockSpec(memory_space=pl.ANY)] + [vmem] * (slabs + 2),
        out_specs=[vmem] * len(chosen),
        out_shape=[jax.ShapeDtypeStruct((len(SHEARS), 4, strip, cols), jnp.bfloat16)] * len(chosen),
        compiler_params=pltpu.CompilerParams(vmem_limit_bytes=VMEM_BYTES),
        name="lit_strips_" + "".join(str(k) for k in chosen),
    )(offsets, after, *[codes[-k % slabs] for k in range(slabs)], sums, opac)


def piece_slots(step, slabs):
    return min(slabs, 2 * PAIR if step < slabs // 2 else PAIR)


def column_swaps(slabs, columns):
    swaps = []
    for step in range(1, slabs // 2 + 1):
        for parity in range(2):
            lefts = [c for c in range(columns - step) if (c // step) % 2 == parity]
            if step > 1 and step == slabs // 2:
                lefts = [c for c in lefts if c > 0]
            if lefts:
                swaps.append((step, parity, lefts))
    return swaps


def swap_columns(value, step, lefts, slabs, columns):
    to = {c: c + step for c in lefts} | {c + step: c for c in lefts}
    rows = lax.axis_size("row")
    pairs = []
    for d in range(slabs):
        for r in range(rows):
            for c in range(columns):
                way = 0 if step == 1 else 0
                there = (d, r, to[c]) if c in to else ((d, r ^ 1, c) if way == 0 else (d ^ way, r, c))
                if there[0] < slabs and there[1] < rows:
                    pairs.append(((d * rows + r) * columns + c, (there[0] * rows + there[1]) * columns + there[2]))
    return lax.ppermute(value, ("depth", "row", "col"), pairs)


def covers(targets_ref, view, slab, column, tile):
    first = targets_ref[view, slab, 0, column]
    return (first == tile) | (first + 1 == tile)


def plan_kernel(slabs, columns, plans, targets_ref, offsets_ref, order_ref, *refs):
    outs = refs[1:]
    mine, column = lax.axis_index("depth"), lax.axis_index("col")
    cols = outs[0].shape[-1]
    shape = (8, cols)
    lane = lax.broadcasted_iota(jnp.int32, shape, 1).astype(jnp.float32)

    def pick(table, row, at):
        rows = lax.broadcasted_iota(jnp.int32, table.shape, 0)
        lanes = lax.broadcasted_iota(jnp.int32, table.shape, 1)
        entry = jnp.where((rows == row) & (lanes == at), table, 0).astype(jnp.float32)
        return jnp.broadcast_to(jnp.sum(jnp.sum(entry, axis=1, keepdims=True), axis=0, keepdims=True), shape)

    def flag(condition):
        return jnp.where(condition, 1.0, 0.0)

    def put(out, at, value):
        out[at] = jnp.concatenate([value, value], axis=0).astype(out.dtype)

    def same(scalar):
        return jnp.full(shape, scalar, jnp.int32).astype(jnp.float32)

    for v in range(len(SHEARS)):
        targets = targets_ref[v, :, 0, :]
        order = [pick(order_ref[...], v, p) for p in range(slabs)]
        slab = [same(origin(mine, k, slabs)) for k in range(slabs)]
        first = [pick(targets, origin(mine, k, slabs), column) for k in range(slabs)]
        offset = [pick(offsets_ref[...], v, origin(mine, k, slabs)) for k in range(slabs)]
        places = [[flag(order[p] == slab[k]) for k in range(slabs)] for p in range(slabs)]

        def columns_of(k, tile):
            return jnp.where(lane >= offset[k], flag(first[k] == tile), flag(first[k] + 1.0 == tile))

        def found_before(firsts, slabs_there, tile):
            count, found = jnp.zeros(shape, jnp.float32), []
            for p in range(slabs):
                here = jnp.zeros(shape, jnp.float32)
                for start, number in zip(firsts, slabs_there, strict=True):
                    covered = flag(start == tile) + flag(start + 1.0 == tile)
                    here = here + flag(order[p] == number) * covered
                found.append((here, count))
                count = count + here
            return found

        for out, (role, step, parity, lefts) in zip(outs, plans, strict=True):
            tile = same(column)
            if role in ("near", "far"):
                is_left = lax.rem(lax.div(column, step), 2) == parity
                is_left = is_left & (column >= lefts[0]) & (column + step < columns)
                is_right = (lax.rem(column, 2) != parity) & (column - step >= lefts[0]) & (step == 1)
                tile = same(jnp.where(is_left, column + step, jnp.where(is_right, column - step, -PAIR)))
            if role == "near":
                for k in range(slabs):
                    put(out, (v, k), columns_of(k, tile))
            elif role == "keep":
                own = [columns_of(k, tile) for k in range(slabs)]
                for p in range(slabs):
                    for k in range(slabs):
                        put(out, (v, p, k), places[p][k] * own[k])
            elif role == "order":
                for p in range(slabs):
                    for k in range(slabs):
                        put(out, (v, p, k), places[p][k])
            elif role == "far":
                found = found_before(first, slab, tile)
                there = [columns_of(k, tile) for k in range(slabs)]
                for slot in range(out.shape[1]):
                    chosen = [here * flag(count == slot) for here, count in found]
                    for k in range(slabs):
                        fits = chosen[0] * places[0][k]
                        for p in range(1, slabs):
                            fits = fits + chosen[p] * places[p][k]
                        put(out, (v, slot, k), fits * there[k])
            elif role == "take":
                source = column - step
                present = same(((source >= 0) & (source < columns)).astype(jnp.int32))
                firsts = [pick(targets, d, source) for d in range(slabs)]
                numbers = [same(d) for d in range(slabs)]
                for p, (here, count) in enumerate(found_before(firsts, numbers, tile)):
                    for slot in range(out.shape[2]):
                        put(out, (v, p, slot), here * present * flag(count == slot))


def piece_plans(targets, offsets, slab_order, columns, after, plans, name):
    slabs = slab_order.shape[1]
    views, cols = len(SHEARS), after.shape[-1]
    vmem = pl.BlockSpec(memory_space=pltpu.VMEM)
    shapes = {"near": lambda n: (slabs,), "far": lambda n: (n, slabs), "take": lambda n: (slabs, n)}
    shapes = [shapes.get(role, lambda n: (slabs, slabs))(piece_slots(step, slabs)) for role, step, _, _ in plans]
    return pl.pallas_call(
        functools.partial(plan_kernel, slabs, columns, plans),
        in_specs=[vmem] * 4,
        out_specs=[vmem] * len(plans),
        out_shape=[pltpu.VMEM((views, *shape, 16, cols), jnp.bfloat16) for shape in shapes],
        compiler_params=pltpu.CompilerParams(vmem_limit_bytes=VMEM_BYTES),
        name=name,
    )(targets, offsets, slab_order, after)


def near_kernel(chosen, outs_count, *refs):
    blocks, masks, outs = refs[: len(chosen)], refs[len(chosen) : -outs_count], refs[-outs_count:]
    for mask_ref, out in zip(masks, outs, strict=True):
        views, _, channels, strip, _ = out.shape
        for v in range(views):
            for i, k in enumerate(chosen):
                mask = mask_ref[v, k]
                for c in range(channels):
                    for row in range(0, strip, 16):
                        rows = pl.ds(row, 16)
                        out[v, i, c, rows] = blocks[i][v, c, rows] * mask


def near_pieces(blocks, masks, chosen, name):
    views, channels, strip, cols = blocks[0].shape
    vmem = pl.BlockSpec(memory_space=pltpu.VMEM)
    return pl.pallas_call(
        functools.partial(near_kernel, chosen, len(masks)),
        in_specs=[vmem] * (len(blocks) + len(masks)),
        out_specs=[vmem] * len(masks),
        out_shape=[jax.ShapeDtypeStruct((views, len(chosen), channels, strip, cols), jnp.bfloat16) for _ in masks],
        compiler_params=pltpu.CompilerParams(vmem_limit_bytes=VMEM_BYTES),
        name=name,
    )(*blocks, *masks)


def pack_kernel(slabs, outs_count, *refs):
    blocks, masks, outs = refs[:slabs], refs[slabs : slabs + outs_count], refs[slabs + outs_count :]
    for mask_ref, out in zip(masks, outs, strict=True):
        views, slots, channels, strip, _ = out.shape
        for v in range(views):
            for slot in range(slots):
                parts = [mask_ref[v, slot, k] for k in range(slabs)]
                for row in range(0, strip, 16):
                    rows = pl.ds(row, 16)
                    for c in range(channels):
                        total = blocks[0][v, c, rows] * parts[0]
                        for k in range(1, slabs):
                            total = total + blocks[k][v, c, rows] * parts[k]
                        out[v, slot, c, rows] = total


def packed_pieces(blocks, masks, name):
    slabs = len(blocks)
    views, channels, strip, cols = blocks[0].shape
    vmem = pl.BlockSpec(memory_space=pltpu.VMEM)
    return pl.pallas_call(
        functools.partial(pack_kernel, slabs, len(masks)),
        in_specs=[vmem] * (slabs + len(masks)),
        out_specs=[vmem] * len(masks),
        out_shape=[
            jax.ShapeDtypeStruct((views, mask.shape[1], channels, strip, cols), jnp.bfloat16) for mask in masks
        ],
        compiler_params=pltpu.CompilerParams(vmem_limit_bytes=VMEM_BYTES),
        name=name,
    )(*blocks, *masks)


def blend_kernel(names, *refs):
    given, out = dict(zip(names, refs[:-1], strict=True)), refs[-1]
    views, slabs, _, strip, cols = out.shape
    order_ref = given["order",]
    tile = lax.axis_index("col")
    near = {parity: [] for parity in range(2)}
    for (kind, *key), ref in given.items():
        if kind == "near":
            near[key[0]].append((key[1], ref))

    def by_strip(groups, v, p, c, rows):
        total = None
        for chosen, ref in groups:
            if not chosen:
                total = ref[v, p, c, rows] if total is None else total + ref[v, p, c, rows]
            for i, k in enumerate(chosen):
                term = ref[v, i, c, rows] * order_ref[v, p, k]
                total = term if total is None else total + term
        return total

    def blend(left, right):
        for v in range(views):
            for p in range(slabs):
                for row in range(0, strip, 16):
                    rows = pl.ds(row, 16)
                    colour = [jnp.zeros((16, cols), jnp.float32) for _ in range(3)]
                    through = jnp.ones((16, cols), jnp.float32)
                    for source in (left, None, right):
                        if source is None:
                            values = [given["own",][v, p, c, rows] for c in range(4)]
                        elif source:
                            values = [by_strip(source, v, p, c, rows) for c in range(4)]
                        else:
                            continue
                        values = [value.astype(jnp.float32) for value in values]
                        for c in range(3):
                            colour[c] = colour[c] + through * values[c]
                        through = through * (1.0 - values[3])
                    for c in range(3):
                        out[v, p, c, rows] = colour[c]
                    out[v, p, 3, rows] = through

    for phase in range(2):
        pl.when(lax.rem(tile, 2) == phase)(functools.partial(blend, near[(phase - 1) % 2], near[phase]))


def ordered_kernel(chosen, order_ref, piece_ref, out):
    views, slabs, channels, strip, _ = out.shape
    for v in range(views):
        for p in range(slabs):
            for c in range(channels):
                for row in range(0, strip, 16):
                    rows = pl.ds(row, 16)
                    total = piece_ref[v, 0, c, rows] * order_ref[v, p, chosen[0]]
                    for i, k in list(enumerate(chosen))[1:]:
                        total = total + piece_ref[v, i, c, rows] * order_ref[v, p, k]
                    out[v, p, c, rows] = total


def ordered_pieces(order, piece, chosen):
    views, _, channels, strip, cols = piece.shape
    vmem = pl.BlockSpec(memory_space=pltpu.VMEM)
    return pl.pallas_call(
        functools.partial(ordered_kernel, chosen),
        in_specs=[vmem, vmem],
        out_specs=vmem,
        out_shape=pltpu.VMEM((views, order.shape[1], channels, strip, cols), jnp.bfloat16),
        compiler_params=pltpu.CompilerParams(vmem_limit_bytes=VMEM_BYTES),
        name="ordered_pieces",
    )(order, piece)


def blended_pieces(given, slabs):
    views, _, channels, strip, cols = given["own",].shape
    vmem = pl.BlockSpec(memory_space=pltpu.VMEM)
    return pl.pallas_call(
        functools.partial(blend_kernel, list(given)),
        in_specs=[vmem] * len(given),
        out_specs=vmem,
        out_shape=pltpu.VMEM((views, slabs, channels, strip, cols), jnp.float32),
        compiler_params=pltpu.CompilerParams(vmem_limit_bytes=VMEM_BYTES),
        name="blend_pieces",
    )(*given.values())


def frame_kernel(names, *refs):
    blended_ref, given = refs[0], dict(zip(names, refs[1:-3], strict=True))
    frame_hbm, frame_ref, sems = refs[-3:]
    views, slabs, _, strip, cols = blended_ref.shape
    tile = lax.axis_index("col")
    steps = sorted({key[1] for key in given if key[0] == "take"}, reverse=True)

    def placed(step, v, p, c, rows):
        arrived = [given["far", step, q] for q in range(2) if ("far", step, q) in given]
        pieces = []
        for ref in arrived:
            total = ref[v, 0, c, rows] * given["take", step][v, p, 0]
            for slot in range(1, ref.shape[1]):
                total = total + ref[v, slot, c, rows] * given["take", step][v, p, slot]
            pieces.append(total)
        first = lax.rem(lax.div(tile + step, step), 2) == 0
        return pieces[0] if len(pieces) == 1 else jnp.where(first, pieces[0], pieces[1])

    copies = []
    for v in range(views):
        for row in range(0, strip, 16):
            rows = pl.ds(row, 16)
            colour = [jnp.zeros((16, cols), jnp.float32) for _ in range(3)]
            weight = jnp.ones((16, cols), jnp.float32)
            for p in range(slabs):
                for step in steps:
                    values = [placed(step, v, p, c, rows).astype(jnp.float32) for c in range(4)]
                    for c in range(3):
                        colour[c] = colour[c] + weight * values[c]
                    weight = weight * (1.0 - values[3])
                for c in range(3):
                    colour[c] = colour[c] + weight * blended_ref[v, p, c, rows]
                weight = weight * blended_ref[v, p, 3, rows]
            for c in range(3):
                frame_ref[v, c, 0, rows] = colour[c]
            frame_ref[v, 3, 0, rows] = 1.0 - weight
        copies.append(pltpu.make_async_copy(frame_ref.at[v], frame_hbm.at[v], sems.at[v]))
        copies[-1].start()
    for copy in copies:
        copy.wait()


def composed_frame(blended, given):
    views, _, channels, strip, cols = blended.shape
    vmem = pl.BlockSpec(memory_space=pltpu.VMEM)
    shape = (views, channels, 1, strip, cols)
    return pl.pallas_call(
        functools.partial(frame_kernel, list(given)),
        in_specs=[vmem] * (1 + len(given)),
        out_specs=pl.BlockSpec(memory_space=pl.ANY),
        out_shape=jax.ShapeDtypeStruct(shape, jnp.float32),
        scratch_shapes=[pltpu.VMEM(shape, jnp.float32), pltpu.SemaphoreType.DMA((views,))],
        compiler_params=pltpu.CompilerParams(vmem_limit_bytes=VMEM_BYTES),
        name="compose_frame",
    )(blended, *given.values())


def on_device(density, albedo, targets, offsets, slab_order):
    depth_cells = density.shape[0]
    slabs, columns = lax.axis_size("depth"), lax.axis_size("col")
    offsets = offsets[:, :, 0, 0]
    code, density = slab_code(density)
    codes = [code] + [swap_depth(code, k, slabs) for k in range(1, slabs)]
    sums, opac = image_sums(density, albedo)
    swaps = column_swaps(slabs, columns)
    near = [swap for swap in swaps if swap[0] == 1]
    far = [swap for swap in swaps if swap[0] > 1]
    far_steps = sorted({swap[0] for swap in far})
    roles = [("near", *swap) for swap in near] + [("far", *swap) for swap in far]
    roles += [("take", step, 0, []) for step in far_steps] + [("keep", 0, 0, []), ("order", 0, 0, [])]
    masks = piece_plans(targets, offsets, slab_order, columns, sums, roles, "piece_plans")
    near_masks, masks = masks[: len(near)], masks[len(near) :]
    strips = {}
    for chosen in (list(range(1, slabs)), [0]):
        lit = lit_strips(codes, sums, opac, offsets, offsets, depth_cells, chosen)
        strips |= dict(zip(chosen, lit, strict=True))
    blocks = {0: strips[0]} | {k: swap_depth(strips[k], k, slabs) for k in range(1, slabs)}
    given = {("order",): masks[-1]}
    given |= {("take", step): mask for step, mask in zip(far_steps, masks[len(far) :], strict=False)}
    for name, chosen in (("early", tuple(range(max(1, slabs // 2)))), ("late", tuple(range(slabs - 1, max(1, slabs // 2) - 1, -1)))):
        pieces = near_pieces([blocks[k] for k in chosen], near_masks, chosen, "near_pieces_" + name)
        for (step, parity, lefts), piece in zip(near, pieces, strict=True):
            given["near", parity, chosen] = swap_columns(piece, step, lefts, slabs, columns)
    blocks = [blocks[k] for k in range(slabs)]
    if far:
        for (step, parity, lefts), piece in zip(far, packed_pieces(blocks, masks[: len(far)], "far_pieces"), strict=True):
            given["far", step, parity] = swap_columns(piece, step, lefts, slabs, columns)
    (given["own",],) = packed_pieces(blocks, masks[-2:-1], "kept_pieces")
    nears = {key: value for key, value in given.items() if key[0] in ("order", "near", "own")}
    fars = {key: value for key, value in given.items() if key not in nears}
    early = tuple(range(max(1, slabs // 2)))
    nears = {
        (("near", key[1], ()) if key[0] == "near" and key[2] == early else key): (
            ordered_pieces(given["order",], value, early) if key[0] == "near" and key[2] == early else value
        )
        for key, value in nears.items()
    }
    return composed_frame(blended_pieces(nears, slabs), fars)


def solution(mesh):
    in_specs = (
        P("depth", "row", "col"),
        P(None, "depth", "row", "col"),
        P(None, None, "row", None),
        P(None, None, "row", "col"),
        P(),
    )
    out_specs = P(None, None, "row", "depth", "col")
    return jax.shard_map(
        on_device, mesh=mesh, in_specs=in_specs, out_specs=out_specs, check_vma=False
    )
```
